256 devices in a mesh: surf: 128 (over z, y, x), wall: 2 (over core).
Axes of the slice: x: 4, y: 4, z: 8, core: 2. Of those that a mesh axis runs over, the one named last changes fastest.
Arguments:
- rhs: float32 [2, 64, 16384], P('wall', None, 'surf'), may hold values from -6 to 6
- prev_solution: float32 [2, 64, 16384], P('wall', None, 'surf'), may hold values from -6 to 6
- lower: float32 [2, 64, 64, 16384], P('wall', None, None, 'surf'), as said below
- pivot_inv: float32 [2, 64, 64, 16384], P('wall', None, None, 'surf'), as said below
- upper_back: float32 [2, 64, 64, 16384], P('wall', None, None, 'surf'), as said below
- coupling: float32 [4, 2, 64, 16384], P(None, 'wall', None, 'surf'), may hold values from -0.5 to 0.5
- neighbours: int32 [4, 16384], P(None, 'surf'), may hold values from 0 to 16383, as said below
- counts: int32 [16384], P('surf'), may hold values from 1 to 2
- colour: int32 [16384], P('surf'), may hold values 0 or 1
Outputs:
- new_solution: float32 [2, 64, 16384], P('wall', None, 'surf')
The draws below stay inside these ranges and needn't reach their ends.
Inputs may be any that keep to these rules, and one draw needn't show every extreme that they name: `neighbours`: each neighbour line is held by the same index of surf as the line, or by the index one below or one above it, cyclically. `lower`: dominant diagonal; the forward recurrence neither grows nor vanishes over a line. `pivot_inv`: dominant diagonal. `upper_back`: dominant diagonal; the backward recurrence neither grows nor vanishes over a line.
All inputs are finite; a program needn't handle non-finite values. No bound on the sum of `colour` on one device may be relied on, other than what follows from the above.
Results may differ from the reference program's by a relative error of at most 0.0001.
Values sent between devices are 32-bit elements; how exact they have to be, the bound alone decides.
A program may use at most 64 MiB of HBM per device.

```python
import math
import jax
import jax.numpy as jnp
from jax import lax

BLOCK = 64
FACES = 4
L_DEV = 128
ROWS = 2
LINES = 16384


def dominant(key, lo, hi, spread, logscale):
    first, second = jax.random.split(key)
    if logscale:
        diag = jnp.exp(jax.random.uniform(first, (ROWS, BLOCK, 1, LINES), jnp.float32, math.log(lo), math.log(hi)))
    else:
        diag = jax.random.uniform(first, (ROWS, BLOCK, 1, LINES), jnp.float32, lo, hi)
    noise = jax.random.normal(second, (ROWS, BLOCK, BLOCK, LINES), jnp.float32) * spread
    eye = (jnp.arange(BLOCK)[:, None] == jnp.arange(BLOCK)[None, :]).astype(jnp.float32)
    return eye[None, :, :, None] * diag + noise


def draw_lower(key, part):
    return dominant(jax.random.fold_in(key, 11), 0.3, 0.97, 0.025, False)


def draw_upper_back(key, part):
    return dominant(jax.random.fold_in(key, 23), 0.3, 0.97, 0.025, False)


def draw_pivot_inv(key, part):
    return dominant(jax.random.fold_in(key, 37), 0.5, 2.0, 0.03, True)


def draw_counts(key, part):
    first, second = jax.random.split(jax.random.fold_in(key, 41))
    values = jax.random.randint(first, (LINES,), 1, ROWS + 1)
    chosen = jax.random.randint(second, (), 0, LINES)
    return jnp.where(jnp.arange(LINES) == chosen, ROWS, values).astype(jnp.int32)


def draw_neighbours(key, part):
    first, second = jax.random.split(jax.random.fold_in(key, 53))
    owners = jnp.arange(LINES, dtype=jnp.int32) // L_DEV
    offsets = jax.random.randint(first, (FACES, LINES), -1, 2)
    within = jax.random.randint(second, (FACES, LINES), 0, L_DEV)
    groups = LINES // L_DEV
    return ((owners[None, :] + offsets + groups) % groups * L_DEV + within).astype(jnp.int32)


def plant(drawn, own_key, low, high):
    longest = drawn.shape.index(max(drawn.shape))
    spots = []
    for shift in (0, 1):
        where = [jax.random.randint(jax.random.fold_in(own_key, axis), (), 0, length) for axis, length in enumerate(drawn.shape)]
        where[longest] = (where[longest] + shift) % drawn.shape[longest]
        spots.append(tuple(where))
    return drawn.at[spots[0]].set(low).at[spots[1]].set(high)


def block_scale(rng, dims, shards, low, largest):
    def one(dim, shards_of):
        steps = jax.random.uniform(jax.random.fold_in(jax.random.fold_in(rng, 6), dim), (shards_of,), jnp.float32, low / len(shards), largest / len(shards))
        return jnp.repeat(jnp.exp(steps), dims[dim] // shards_of).reshape((-1,) + (1,) * (len(dims) - dim - 1))

    level = one(*shards[0])
    for cut in shards[1:]:
        level = level * one(*cut)
    return level


def normal_values(key, extent, scale, most, shards=(), kind=jnp.bfloat16):
    drawn = scale * jax.random.normal(key, extent, jnp.float32)
    if shards:
        drawn = drawn * block_scale(key, extent, shards, -0.22, 0.18)
    return jnp.clip(drawn, -most, most).astype(kind)


def setup_inputs(seed: int = 0) -> dict:
    key_of = jax.random.split(jax.random.key(seed), 10)
    rhs = normal_values(key_of[0], (ROWS, BLOCK, LINES), 1.0, 6.0, ((0, 2), (2, 128)), jnp.float32)
    prev_solution = normal_values(key_of[1], (ROWS, BLOCK, LINES), 1.0, 6.0, ((0, 2), (2, 128)), jnp.float32)
    lower = draw_lower(jax.random.fold_in(key_of[9], 71), 0)
    pivot_inv = draw_pivot_inv(jax.random.fold_in(key_of[9], 71), 0)
    upper_back = draw_upper_back(jax.random.fold_in(key_of[9], 71), 0)
    coupling = jnp.clip(jax.random.uniform(key_of[5], (FACES, ROWS, BLOCK, LINES), jnp.float32, -0.5, 0.5) * block_scale(key_of[5], (FACES, ROWS, BLOCK, LINES), ((1, 2), (3, 128)), -0.4, 0.0), -0.5, 0.5)
    neighbours = draw_neighbours(jax.random.fold_in(key_of[9], 71), 0)
    counts = draw_counts(jax.random.fold_in(key_of[9], 71), 0)
    colour = plant((jax.random.randint(key_of[8], (LINES,), 0, 2) < 1).astype(jnp.int32), jax.random.fold_in(key_of[8], 1), 0, 1)
    return {"rhs": rhs, "prev_solution": prev_solution, "lower": lower, "pivot_inv": pivot_inv, "upper_back": upper_back, "coupling": coupling, "neighbours": neighbours, "counts": counts, "colour": colour}


def matvec(mat, vec):
    return jnp.einsum("abl,bl->al", mat, vec, precision=lax.Precision.HIGHEST)


def reference(rhs, prev_solution, lower, pivot_inv, upper_back, coupling, neighbours, counts, colour):
    active = (jnp.arange(ROWS, dtype=jnp.int32)[:, None] < counts[None, :]).astype(jnp.float32)
    zeros = jnp.zeros((BLOCK, LINES), jnp.float32)

    def line_solve(source):
        def forward(carry, items):
            mat, value, mask = items
            result = mask[None, :] * (value - matvec(mat, carry))
            return result, result

        _, ys = lax.scan(forward, zeros, (lower, source, active))

        def backward(carry, items):
            inv, back, value, mask = items
            result = mask[None, :] * (matvec(inv, value) - matvec(back, carry))
            return result, result

        _, xs = lax.scan(backward, zeros, (pivot_inv, upper_back, ys, active), reverse=True)
        return xs

    def source_of(field):
        total = rhs
        for face in range(FACES):
            total = total - coupling[face] * jnp.take(field, neighbours[face], axis=2)
        return total

    first = line_solve(source_of(prev_solution))
    current = jnp.where((colour == 0)[None, None, :], first, prev_solution)
    second = line_solve(source_of(current))
    return jnp.where((colour == 1)[None, None, :], second, current)
```

```python
import functools

import jax
import jax.numpy as jnp
from jax import lax
from jax.experimental import pallas as pl
from jax.experimental.pallas import tpu as pltpu
from jax.sharding import PartitionSpec as P

MESH = pl.DeviceIdType.MESH
BLOCK = 64
FACES = 4
LANES = 128
SUB = 8
TILES = BLOCK // SUB


def tile(j):
    return pl.ds(pl.multiple_of(j * SUB, SUB), SUB)


def fold(parts, masks):
    step = 1
    for mask in masks:
        merged = []
        for base in range(0, len(parts), 2):
            a, b = parts[base], parts[base + 1]
            merged.append(jnp.where(mask, a, b) + pltpu.roll(jnp.where(mask, b, a), step, 0))
        parts = merged
        step *= 2
    return parts[0]


def tree(terms):
    while len(terms) > 1:
        terms = [terms[i] + terms[i + 1] for i in range(0, len(terms) - 1, 2)] + terms[len(terms) & ~1:]
    return terms[0]


def products(pairs, finish, masks):
    vecs = [[vec[pl.ds(SUB * b, SUB), :] for b in range(TILES)] for _, vec in pairs]

    def body(j, _):
        parts = []
        for a in range(SUB):
            row = j * SUB + a
            terms = []
            for (mat, _), vec in zip(pairs, vecs):
                terms.append(tree([mat[row, pl.ds(SUB * b, SUB), :] * vec[b] for b in range(TILES)]))
            parts.append(terms[0] if len(terms) == 1 else terms[0] - terms[1])
        finish(j, fold(parts, masks))
        return 0

    lax.fori_loop(0, TILES, body, 0)


def kernel(groups, rhs, prev, lower, pivot, upper, coupling, neighbours, counts, colour, out,
           lo, p1, p0, up, v0, v1, r0, r1, c0, c1, nb, cnt, col, h1, h2, f0, f1, x0, x1, cur0, cur1, gy, gx, gc,
           loc, wsend, wrecv, s1, q1, s2, q2):
    s = lax.axis_index("surf")
    w = lax.axis_index("wall")
    right = lax.rem(s + 1, groups)
    left = lax.rem(s + groups - 1, groups)
    sub = lax.broadcasted_iota(jnp.int32, (SUB, LANES), 0)
    masks = [(sub & 1) == 0, (sub & 2) == 0, (sub & 4) == 0]
    barrier = pltpu.get_barrier_semaphore()

    def wall_copy(src, dst, i, to):
        return pltpu.make_async_remote_copy(src_ref=src, dst_ref=dst, send_sem=wsend.at[i], recv_sem=wrecv.at[i],
                                            device_id=(s, to), device_id_type=MESH)

    down = [
        wall_copy(prev.at[0], v0, 0, 1),
        wall_copy(rhs.at[0], r0, 1, 1),
        wall_copy(coupling.at[:, 0], c0, 2, 1),
        wall_copy(pivot.at[0], p0, 3, 1),
        wall_copy(upper.at[0], up, 4, 1),
    ]
    back_cur = wall_copy(cur0, gc, 5, 0)
    back_y = wall_copy(f0, gy, 6, 0)
    back_x = wall_copy(x1, gx, 7, 0)

    def local(src, dst, i):
        return pltpu.make_async_copy(src, dst, loc.at[i])

    @pl.when(w == 0)
    def _():
        pl.semaphore_signal(barrier, inc=1, device_id=(s, 1), device_id_type=MESH)
        pl.semaphore_wait(barrier, 1)
        for c in down:
            c.start()
        mine = [local(pivot.at[0], p0, 0), local(upper.at[0], up, 1), local(colour, col, 2), local(counts, cnt, 3)]
        for c in mine:
            c.start()
        for c in mine:
            c.wait()
        back_cur.wait_recv()
        back_y.wait_recv()

        def keep(j, t):
            f1[tile(j), :] = t

        products([(p0, gy)], keep, masks)
        second = jnp.broadcast_to(col[...] == 1, (SUB, LANES))
        alive = jnp.broadcast_to((cnt[...] > 0).astype(jnp.float32), (SUB, LANES))
        back_x.wait_recv()

        def last(j, t):
            out[0, tile(j), :] = jnp.where(second, alive * (f1[tile(j), :] - t), gc[tile(j), :])

        products([(up, gx)], last, masks)
        for c in down:
            c.wait_send()

    @pl.when(w == 1)
    def _():
        pl.semaphore_signal(barrier, inc=1, device_id=(s, 0), device_id_type=MESH)
        pl.semaphore_signal(barrier, inc=1, device_id=(right, 1), device_id_type=MESH)
        pl.semaphore_signal(barrier, inc=1, device_id=(left, 1), device_id_type=MESH)
        mine = [local(prev.at[0], v1, 0), local(rhs.at[0], r1, 1), local(coupling.at[:, 0], c1, 2),
                local(neighbours, nb, 3), local(counts, cnt, 4), local(colour, col, 5),
                local(lower.at[0], lo, 6), local(pivot.at[0], p1, 7)]
        for c in mine:
            c.start()
        pl.semaphore_wait(barrier, 3)

        def surf_copy(src, buf, send, recv, side, row):
            return pltpu.make_async_remote_copy(
                src_ref=src, dst_ref=buf.at[side, row], send_sem=send.at[side, row], recv_sem=recv.at[side, row],
                device_id=(right if side == 0 else left, 1), device_id_type=MESH)

        first = [[surf_copy(v, h1, s1, q1, side, row) for row, v in ((0, v0), (1, v1))] for side in (0, 1)]
        again = [[surf_copy(v, h2, s2, q2, side, row) for row, v in ((0, cur0), (1, cur1))] for side in (0, 1)]
        mine[0].wait()
        first[0][1].start()
        first[1][1].start()
        down[0].wait_recv()
        first[0][0].start()
        first[1][0].start()
        for c in mine[1:6]:
            c.wait()
        down[1].wait_recv()
        down[2].wait_recv()

        here = []
        above = []
        below = []
        lanes = []
        for k in range(FACES):
            line = nb[pl.ds(k, 1), :]
            lanes.append(jnp.broadcast_to(line & (LANES - 1), (SUB, LANES)))
            owner = jnp.broadcast_to(line >> 7, (SUB, LANES))
            here.append(owner == s)
            above.append(owner == right)
            below.append(owner == left)
        alive0 = jnp.broadcast_to((cnt[...] > 0).astype(jnp.float32), (SUB, LANES))
        alive1 = jnp.broadcast_to((cnt[...] > 1).astype(jnp.float32), (SUB, LANES))
        colours = jnp.broadcast_to(col[...], (SUB, LANES))
        rows = ((r0, c0, f0), (r1, c1, f1))

        def pick(value, lane):
            return jnp.take_along_axis(value, lane, axis=1, mode="promise_in_bounds")

        def own_part(fields):
            def body(j, _):
                for (rr, cc, ff), field in zip(rows, fields):
                    total = rr[tile(j), :]
                    value = field[tile(j), :]
                    for k in range(FACES):
                        total = total - cc[k, tile(j), :] * jnp.where(here[k], pick(value, lanes[k]), 0.0)
                    ff[tile(j), :] = total
                return 0

            lax.fori_loop(0, TILES, body, 0)

        def far_part(halo):
            def body(j, _):
                for row, (rr, cc, ff) in enumerate(rows):
                    total = ff[tile(j), :]
                    lval = halo[0, row, tile(j), :]
                    rval = halo[1, row, tile(j), :]
                    for k in range(FACES):
                        far = jnp.where(above[k], pick(rval, lanes[k]),
                                        jnp.where(below[k], pick(lval, lanes[k]), 0.0))
                        total = total - cc[k, tile(j), :] * far
                    ff[tile(j), :] = total * alive0 if row == 0 else total
                return 0

            lax.fori_loop(0, TILES, body, 0)

        def forward(j, t):
            f1[tile(j), :] = alive1 * (f1[tile(j), :] - t)

        def solved1(j, t):
            x1[tile(j), :] = alive1 * t

        own_part((v0, v1))
        mine[6].wait()
        mine[7].wait()
        for row in (1, 0):
            for side in (0, 1):
                first[side][row].wait_recv()
        far_part(h1)
        products([(lo, f0)], forward, masks)

        def first1(j, t):
            cur1[tile(j), :] = jnp.where(colours == 0, alive1 * t, v1[tile(j), :])

        def solved1_full(j, t):
            x1[tile(j), :] = alive1 * t
            first1(j, t)

        products([(p1, f1)], solved1_full, masks)
        again[0][1].start()
        again[1][1].start()
        down[3].wait_recv()
        down[4].wait_recv()

        def first0(j, t):
            cur0[tile(j), :] = jnp.where(colours == 0, alive0 * t, v0[tile(j), :])

        products([(p0, f0), (up, x1)], first0, masks)
        again[0][0].start()
        again[1][0].start()
        back_cur.start()
        own_part((cur0, cur1))
        for row in (1, 0):
            for side in (0, 1):
                again[side][row].wait_recv()
        far_part(h2)
        back_y.start()
        products([(lo, f0)], forward, masks)
        products([(p1, f1)], solved1, masks)
        back_x.start()

        def body(j, _):
            out[0, tile(j), :] = jnp.where(colours == 1, x1[tile(j), :], cur1[tile(j), :])
            return 0

        lax.fori_loop(0, TILES, body, 0)
        for pair in first + again:
            for c in pair:
                c.wait_send()
        back_cur.wait_send()
        back_y.wait_send()
        back_x.wait_send()


def shards(groups, rhs, prev_solution, lower, pivot_inv, upper_back, coupling, neighbours, counts, colour):
    plane = pltpu.VMEM((BLOCK, LANES), jnp.float32)
    matrix = pltpu.VMEM((BLOCK, BLOCK, LANES), jnp.float32)
    faces = pltpu.VMEM((FACES, BLOCK, LANES), jnp.float32)
    halo = pltpu.VMEM((2, 2, BLOCK, LANES), jnp.float32)
    line = pltpu.VMEM((1, LANES), jnp.int32)
    dma = pltpu.SemaphoreType.DMA
    return pl.pallas_call(
        functools.partial(kernel, groups),
        out_shape=jax.ShapeDtypeStruct((1, BLOCK, LANES), jnp.float32),
        in_specs=[pl.BlockSpec(memory_space=pltpu.HBM)] * 9,
        out_specs=pl.BlockSpec(memory_space=pltpu.VMEM),
        scratch_shapes=[matrix] * 4 + [plane] * 4 + [faces] * 2
        + [pltpu.VMEM((FACES, LANES), jnp.int32), line, line] + [halo] * 2 + [plane] * 9
        + [dma((8,)), dma((8,)), dma((8,))] + [dma((2, 2))] * 4,
        compiler_params=pltpu.CompilerParams(collective_id=0, has_side_effects=True, vmem_limit_bytes=56 << 20),
    )(rhs, prev_solution, lower, pivot_inv, upper_back, coupling, neighbours,
      counts.reshape(1, LANES), colour.reshape(1, LANES))


def solution(mesh):
    placed = (
        P("wall", None, "surf"),
        P("wall", None, "surf"),
        P("wall", None, None, "surf"),
        P("wall", None, None, "surf"),
        P("wall", None, None, "surf"),
        P(None, "wall", None, "surf"),
        P(None, "surf"),
        P("surf"),
        P("surf"),
    )
    return jax.shard_map(
        functools.partial(shards, mesh.shape["surf"]), mesh=mesh, in_specs=placed, out_specs=P("wall", None, "surf"),
        check_vma=False,
    )
```

```python
import functools

import jax
import jax.numpy as jnp
from jax import lax
from jax.experimental import pallas as pl
from jax.experimental.pallas import tpu as pltpu
from jax.sharding import PartitionSpec as P

MESH = pl.DeviceIdType.MESH
BLOCK = 64
FACES = 4
LANES = 128
SUB = 8
TILES = BLOCK // SUB
ROW = 4
PLANE = 16


def tile(j):
    return pl.ds(pl.multiple_of(j * SUB, SUB), SUB)


def fold(parts, masks):
    step = 1
    for mask in masks:
        merged = []
        for base in range(0, len(parts), 2):
            a, b = parts[base], parts[base + 1]
            merged.append(jnp.where(mask, a, b) + pltpu.roll(jnp.where(mask, b, a), step, 0))
        parts = merged
        step *= 2
    return parts[0]


def tree(terms):
    while len(terms) > 1:
        terms = [terms[i] + terms[i + 1] for i in range(0, len(terms) - 1, 2)] + terms[len(terms) & ~1:]
    return terms[0]


def products(pairs, finish, masks):
    vecs = [[vec[pl.ds(SUB * b, SUB), :] for b in range(TILES)] for _, vec in pairs]

    def body(j, _):
        parts = []
        for a in range(SUB):
            row = j * SUB + a
            terms = []
            for (mat, _), vec in zip(pairs, vecs):
                terms.append(tree([mat[row, pl.ds(SUB * b, SUB), :] * vec[b] for b in range(TILES)]))
            parts.append(terms[0] if len(terms) == 1 else terms[0] - terms[1])
        finish(j, fold(parts, masks))
        return 0

    lax.fori_loop(0, TILES, body, 0, unroll=TILES)


def kernel(groups, rhs, prev, lower, pivot, upper, coupling, neighbours, counts, colour, out,
           mat_a, mat_b, v0, v1, r0, r1, c0, c1, nb, cnt, col, h1, h2, f0, f1, x1, cur0, cur1, gy, gx, held, hop,
           loc, wsend, wrecv, s1, q1, s2, q2, rsend, rrecv, ready):
    s = lax.axis_index("surf")
    w = lax.axis_index("wall")
    right = lax.rem(s + 1, groups)
    left = lax.rem(s + groups - 1, groups)
    place = lax.rem(s, ROW)
    last_line = groups - 1
    sub = lax.broadcasted_iota(jnp.int32, (SUB, LANES), 0)
    masks = [(sub & 1) == 0, (sub & 2) == 0, (sub & 4) == 0]
    barrier = pltpu.get_barrier_semaphore()

    def signal(sem, to, core):
        pl.semaphore_signal(sem, inc=1, device_id=(to, core), device_id_type=MESH)

    def local(src, dst, i):
        return pltpu.make_async_copy(src, dst, loc.at[i])

    def wall_copy(src, dst, i, to):
        return pltpu.make_async_remote_copy(src_ref=src, dst_ref=dst, send_sem=wsend.at[i], recv_sem=wrecv.at[i],
                                            device_id=(s, to), device_id_type=MESH)

    def surf_copy(src, buf, send, recv, side, row):
        return pltpu.make_async_remote_copy(
            src_ref=src, dst_ref=buf.at[side, row], send_sem=send.at[side], recv_sem=recv.at[side, row],
            device_id=(right if side == 0 else left, 1), device_id_type=MESH)

    down = [wall_copy(prev.at[0], v0, 0, 1), wall_copy(rhs.at[0], r0, 1, 1), wall_copy(coupling.at[:, 0], c0, 2, 1)]
    down_cur = wall_copy(cur0, held, 3, 1)
    back_y = [wall_copy(f0.at[i], gy.at[i], 4 + i, 0) for i in (0, 1)]
    back_x = [wall_copy(x1.at[i], gx.at[i], 6 + i, 0) for i in (0, 1)]

    def send_prev(row, copies):
        copies[0].start()

        @pl.when((s != 0) & ((s != last_line) | (row == 0)))
        def _():
            copies[1].start()

    step1, step2 = ROW - 1, PLANE - 1

    def relay(src, dst, row, to, recv):
        return pltpu.make_async_remote_copy(
            src_ref=src, dst_ref=dst, send_sem=rsend.at[row], recv_sem=recv, device_id=(to, 1), device_id_type=MESH)

    start = [relay(prev.at[0], hop.at[row], row, step1, rrecv.at[row]) for row in (0, 1)]
    middle = [relay(hop.at[row], hop.at[row], row, step2, rrecv.at[row]) for row in (0, 1)]
    end = [relay(hop.at[row], h1.at[1, row], row, last_line, q1.at[1, row]) for row in (0, 1)]

    def finish_sends(first, again):
        for c in [first[0]] + again:
            c.wait_send()

        @pl.when(s != 0)
        def _():
            first[1].wait_send()

    @pl.when(w == 0)
    def _():
        mine = [local(prev.at[0], v0, 0), local(colour, col, 1), local(counts, cnt, 2),
                local(pivot.at[0], mat_a, 3), local(upper.at[0], mat_b, 4)]
        pl.semaphore_wait(barrier, 3)

        @pl.when(s == 0)
        def _():
            start[0].start()

        first = [surf_copy(prev.at[0], h1, s1, q1, side, 0) for side in (0, 1)]
        again = [surf_copy(cur0, h2, s2, q2, side, 0) for side in (0, 1)]
        send_prev(0, first)
        for c in down:
            c.start()
        for c in mine:
            c.start()
        for c in mine:
            c.wait()
        alive = jnp.broadcast_to((cnt[...] > 0).astype(jnp.float32), (SUB, LANES))
        colours = jnp.broadcast_to(col[...], (SUB, LANES))

        def keep(j, t):
            held[tile(j), :] = t

        def first0(j, t):
            cur0[tile(j), :] = jnp.where(colours == 0, alive * (held[tile(j), :] - t), v0[tile(j), :])

        def second0(j, t):
            out[0, tile(j), :] = jnp.where(colours == 1, alive * (held[tile(j), :] - t), cur0[tile(j), :])

        back_y[0].wait_recv()
        products([(mat_a, gy.at[0])], keep, masks)
        back_x[0].wait_recv()
        products([(mat_b, gx.at[0])], first0, masks)
        for c in again:
            c.start()
        down_cur.start()
        back_y[1].wait_recv()
        products([(mat_a, gy.at[1])], keep, masks)
        back_x[1].wait_recv()
        products([(mat_b, gx.at[1])], second0, masks)
        finish_sends(first, again + down + [down_cur])

        @pl.when(s == 0)
        def _():
            start[0].wait_send()


    @pl.when(w == 1)
    def _():
        def greet(to, core):
            signal(barrier, to, core)

        greet(s, 0)
        greet(left, 0)
        greet(left, 1)

        @pl.when(s != last_line)
        def _():
            greet(right, 0)

        @pl.when(s < last_line - 1)
        def _():
            greet(right, 1)

        @pl.when(s == step1)
        def _():
            greet(0, 0)
            greet(0, 1)
            greet(step2, 1)

        @pl.when(s == step2)
        def _():
            greet(last_line, 1)

        mine = [local(prev.at[0], v1, 0), local(rhs.at[0], r1, 1), local(coupling.at[:, 0], c1, 2),
                local(neighbours, nb, 3), local(counts, cnt, 4), local(colour, col, 5),
                local(lower.at[0], mat_a, 6), local(pivot.at[0], mat_b, 7)]
        ends = (s == 0) | (s == last_line)
        pl.semaphore_wait(barrier, jnp.where(ends, 1, 2) + jnp.where(ends | (s == step2), 1, 0))

        @pl.when(s == last_line)
        def _():
            signal(ready.at[0], step2, 1)

        @pl.when(s == step2)
        def _():
            signal(ready.at[0], step1, 1)

        @pl.when(s == last_line - 1)
        def _():
            signal(ready.at[1], last_line, 1)

        @pl.when(s == 0)
        def _():
            start[1].start()

        first = [surf_copy(prev.at[0], h1, s1, q1, side, 1) for side in (0, 1)]
        again = [surf_copy(cur1, h2, s2, q2, side, 1) for side in (0, 1)]
        send_prev(1, first)
        for c in mine:
            c.start()

        @pl.when(s == last_line)
        def _():
            pl.semaphore_wait(ready.at[1], 1)
            first[1].start()

        def pass_on(arriving, leaving):
            pl.semaphore_wait(ready.at[0], 1)
            for row in (0, 1):
                arriving[row].wait_recv()
                leaving[row].start()

        @pl.when(s == step1)
        def _():
            pass_on(start, middle)

        @pl.when(s == step2)
        def _():
            pass_on(middle, end)

        mine[0].wait()
        down[0].wait_recv()
        for c in mine[1:6]:
            c.wait()
        down[1].wait_recv()
        down[2].wait_recv()

        slow = jnp.where(place == ROW - 1, 1, 0)
        quick = 1 - slow
        slow_line = jnp.where(slow == 1, right, left)
        quick_line = jnp.where(slow == 1, left, right)
        owners = ([], [], [])
        lanes = []
        for k in range(FACES):
            line = nb[pl.ds(k, 1), :]
            lanes.append(jnp.broadcast_to(line & (LANES - 1), (SUB, LANES)))
            owner = jnp.broadcast_to(line >> 7, (SUB, LANES))
            for masks_of, holder in zip(owners, (s, quick_line, slow_line)):
                masks_of.append(owner == holder)
        here, near, far = owners
        alive0 = jnp.broadcast_to((cnt[...] > 0).astype(jnp.float32), (SUB, LANES))
        alive1 = jnp.broadcast_to((cnt[...] > 1).astype(jnp.float32), (SUB, LANES))
        colours = jnp.broadcast_to(col[...], (SUB, LANES))
        coef = (c0, c1)

        def minus(start, row, j, value, held_by):
            for k in range(FACES):
                taken = jnp.take_along_axis(value, lanes[k], axis=1, mode="promise_in_bounds")
                start = start - coef[row][k, tile(j), :] * jnp.where(held_by[k], taken, 0.0)
            return start

        def own_part(total, given, row, field):
            def body(j, _):
                total[tile(j), :] = minus(given[tile(j), :], row, j, field[tile(j), :], here)
                return 0

            lax.fori_loop(0, TILES, body, 0, unroll=TILES)

        def side_part(total, halo, side, held_by, row, scale):
            def body(j, _):
                value = minus(total[tile(j), :], row, j, halo[side, row, tile(j), :], held_by)
                total[tile(j), :] = value if scale is None else scale * value
                return 0

            lax.fori_loop(0, TILES, body, 0, unroll=TILES)

        def wait(buf, recv, side, row):
            pltpu.make_async_copy(buf.at[side, row], buf.at[side, row], recv.at[side, row]).wait()

        def solve(phase, halo, recv, finish):
            y0 = f0.at[phase]
            for row, total in ((1, f1), (0, y0)):
                wait(halo, recv, quick, row)
                side_part(total, halo, quick, near, row, None)
            wait(halo, recv, slow, 1)
            wait(halo, recv, slow, 0)
            side_part(y0, halo, slow, far, 0, alive0)
            back_y[phase].start()

            def forward(j, t):
                source = minus(f1[tile(j), :], 1, j, halo[slow, 1, tile(j), :], far)
                f1[tile(j), :] = alive1 * (source - t)

            products([(mat_a, y0)], forward, masks)
            products([(mat_b, f1)], finish, masks)
            back_x[phase].start()

        def first1(j, t):
            x1[0, tile(j), :] = alive1 * t
            cur1[tile(j), :] = jnp.where(colours == 0, alive1 * t, v1[tile(j), :])

        def second1(j, t):
            x1[1, tile(j), :] = alive1 * t
            out[0, tile(j), :] = jnp.where(colours == 1, alive1 * t, cur1[tile(j), :])

        own_part(f0.at[0], r0, 0, v0)
        own_part(f1, r1, 1, v1)
        mine[6].wait()
        mine[7].wait()
        solve(0, h1, q1, first1)
        for c in again:
            c.start()
        own_part(f1, r1, 1, cur1)
        down_cur.wait_recv()
        own_part(f0.at[1], r0, 0, held)
        solve(1, h2, q2, second1)
        finish_sends(first, again + back_y + back_x)

        @pl.when(s == 0)
        def _():
            start[1].wait_send()

        @pl.when(s == step1)
        def _():
            for c in middle:
                c.wait_send()

        @pl.when(s == step2)
        def _():
            for c in end:
                c.wait_send()


def shards(groups, rhs, prev_solution, lower, pivot_inv, upper_back, coupling, neighbours, counts, colour):
    plane = pltpu.VMEM((BLOCK, LANES), jnp.float32)
    matrix = pltpu.VMEM((BLOCK, BLOCK, LANES), jnp.float32)
    faces = pltpu.VMEM((FACES, BLOCK, LANES), jnp.float32)
    halo = pltpu.VMEM((2, 2, BLOCK, LANES), jnp.float32)
    pair = pltpu.VMEM((2, BLOCK, LANES), jnp.float32)
    line = pltpu.VMEM((1, LANES), jnp.int32)
    dma = pltpu.SemaphoreType.DMA
    here = (rhs, prev_solution, lower, pivot_inv, upper_back, coupling, neighbours,
            counts.reshape(1, LANES), colour.reshape(1, LANES))
    return pl.pallas_call(
        functools.partial(kernel, groups),
        out_shape=pltpu.VMEM((1, BLOCK, LANES), jnp.float32),
        in_specs=[pl.BlockSpec(memory_space=pltpu.HBM)] * 9,
        out_specs=pl.BlockSpec(memory_space=pltpu.VMEM),
        scratch_shapes=[matrix] * 2 + [plane] * 4 + [faces] * 2
        + [pltpu.VMEM((FACES, LANES), jnp.int32), line, line] + [halo] * 2
        + [pair, plane, pair, plane, plane, pair, pair, plane, pair]
        + [dma((8,)), dma((8,)), dma((8,))] + [dma((2,)), dma((2, 2))] * 2
        + [dma((2,)), dma((2,)), pltpu.SemaphoreType.REGULAR((2,))],
        compiler_params=pltpu.CompilerParams(collective_id=0, has_side_effects=True, vmem_limit_bytes=16 << 20),
    )(*[pltpu.with_memory_space_constraint(a, pltpu.HBM) for a in here])


def solution(mesh):
    placed = (
        P("wall", None, "surf"),
        P("wall", None, "surf"),
        P("wall", None, None, "surf"),
        P("wall", None, None, "surf"),
        P("wall", None, None, "surf"),
        P(None, "wall", None, "surf"),
        P(None, "surf"),
        P("surf"),
        P("surf"),
    )
    return jax.shard_map(
        functools.partial(shards, mesh.shape["surf"]), mesh=mesh, in_specs=placed, out_specs=P("wall", None, "surf"),
        check_vma=False,
    )
```

```python
import functools

import jax
import jax.numpy as jnp
from jax import lax
from jax.experimental import pallas as pl
from jax.experimental.pallas import tpu as pltpu
from jax.sharding import PartitionSpec as P

MESH = pl.DeviceIdType.MESH
BLOCK = 64
FACES = 4
LANES = 128
SUB = 8
TILES = BLOCK // SUB
ROW = 4
PLANE = 16


def tile(j):
    return pl.ds(pl.multiple_of(j * SUB, SUB), SUB)


def fold(parts, masks):
    step = 1
    for mask in masks:
        merged = []
        for base in range(0, len(parts), 2):
            a, b = parts[base], parts[base + 1]
            merged.append(jnp.where(mask, a, b) + pltpu.roll(jnp.where(mask, b, a), step, 0))
        parts = merged
        step *= 2
    return parts[0]


def tree(terms):
    while len(terms) > 1:
        terms = [terms[i] + terms[i + 1] for i in range(0, len(terms) - 1, 2)] + terms[len(terms) & ~1:]
    return terms[0]


def products(pairs, finish, masks):
    vecs = [[vec[pl.ds(SUB * b, SUB), :] for b in range(TILES)] for _, vec in pairs]

    def body(j, _):
        parts = []
        for a in range(SUB):
            row = j * SUB + a
            terms = []
            for (mat, _), vec in zip(pairs, vecs):
                terms.append(tree([mat[row, pl.ds(SUB * b, SUB), :] * vec[b] for b in range(TILES)]))
            parts.append(terms[0] if len(terms) == 1 else terms[0] - terms[1])
        finish(j, fold(parts, masks))
        return 0

    lax.fori_loop(0, TILES, body, 0, unroll=TILES)


def kernel(groups, rhs, prev, lower, pivot, upper, coupling, neighbours, counts, colour, out,
           mat_l, mat_p1, mat_p0, mat_u, v0, v1, r0, r1, c0, c1, nb, cnt, col, h1, h2, f0, f1, x1, cur0, cur1, part_t, part_u,
           got_y, got_x, hop, loc, wsend, wrecv, s1, q1, s2, q2, rsend, rrecv, ready):
    s = lax.axis_index("surf")
    w = lax.axis_index("wall")
    right = lax.rem(s + 1, groups)
    left = lax.rem(s + groups - 1, groups)
    place = lax.rem(s, ROW)
    last_line = groups - 1
    sub = lax.broadcasted_iota(jnp.int32, (SUB, LANES), 0)
    masks = [(sub & 1) == 0, (sub & 2) == 0, (sub & 4) == 0]
    barrier = pltpu.get_barrier_semaphore()
    slow = jnp.where(place == ROW - 1, 1, 0)
    quick = 1 - slow
    slow_line = jnp.where(slow == 1, right, left)
    quick_line = jnp.where(slow == 1, left, right)

    def signal(sem, to, core):
        pl.semaphore_signal(sem, inc=1, device_id=(to, core), device_id_type=MESH)

    def local(src, dst, i):
        return pltpu.make_async_copy(src, dst, loc.at[i])

    def wall_copy(src, dst, i, to):
        return pltpu.make_async_remote_copy(src_ref=src, dst_ref=dst, send_sem=wsend.at[i], recv_sem=wrecv.at[i],
                                            device_id=(s, to), device_id_type=MESH)

    def first_copy(side, row):
        return pltpu.make_async_remote_copy(
            src_ref=prev.at[0], dst_ref=h1.at[side, row], send_sem=s1.at[side], recv_sem=q1.at[side, row],
            device_id=(right if side == 0 else left, 1), device_id_type=MESH)

    def again_copy(src, kind, side, core):
        return pltpu.make_async_remote_copy(
            src_ref=src, dst_ref=h2.at[side, kind], send_sem=s2.at[kind, side, core], recv_sem=q2.at[side, kind],
            device_id=(right if side == 0 else left, core), device_id_type=MESH)

    def again_copies(src, kind, core):
        return [again_copy(src, kind, side, core) for side in (0, 1)]

    down = [wall_copy(prev.at[0], v0, 0, 1), wall_copy(rhs.at[0], r0, 1, 1), wall_copy(coupling.at[:, 0], c0, 2, 1),
            wall_copy(upper.at[0], mat_u, 3, 1)]
    down_t = wall_copy(part_t, part_t, 4, 1)
    up = [wall_copy(rhs.at[0], r1, 5, 0), wall_copy(coupling.at[:, 0], c1, 6, 0), wall_copy(lower.at[0], mat_l, 7, 0),
          wall_copy(pivot.at[0], mat_p1, 8, 0)]
    up_cur = wall_copy(cur1, cur1, 9, 0)
    up_y = wall_copy(f0.at[0], got_y, 10, 0)
    up_x = wall_copy(x1, got_x, 11, 0)

    def start_slow_first(copies):
        @pl.when(place == 0)
        def _():
            copies[1].start()
            copies[0].start()

        @pl.when(place != 0)
        def _():
            copies[0].start()
            copies[1].start()

    def send_prev(row, copies):
        copies[0].start()

        @pl.when((s != 0) & ((s != last_line) | (row == 0)))
        def _():
            copies[1].start()

    step1, step2 = ROW - 1, PLANE - 1

    def relay(src, dst, row, to, recv):
        return pltpu.make_async_remote_copy(
            src_ref=src, dst_ref=dst, send_sem=rsend.at[row], recv_sem=recv, device_id=(to, 1), device_id_type=MESH)

    start = [relay(prev.at[0], hop.at[row], row, step1, rrecv.at[row]) for row in (0, 1)]
    middle = [relay(hop.at[row], hop.at[row], row, step2, rrecv.at[row]) for row in (0, 1)]
    end = [relay(hop.at[row], h1.at[1, row], row, last_line, q1.at[1, row]) for row in (0, 1)]

    def finish_sends(first, others):
        for c in [first[0]] + others:
            c.wait_send()

        @pl.when(s != 0)
        def _():
            first[1].wait_send()

    def arrived(buf, recv, side, kind):
        pltpu.make_async_copy(buf.at[side, kind], buf.at[side, kind], recv.at[side, kind]).wait()

    def make_solver():
        owners = ([], [], [])
        lanes = []
        for k in range(FACES):
            line = nb[pl.ds(k, 1), :]
            lanes.append(jnp.broadcast_to(line & (LANES - 1), (SUB, LANES)))
            owner = jnp.broadcast_to(line >> 7, (SUB, LANES))
            for masks_of, holder in zip(owners, (s, quick_line, slow_line)):
                masks_of.append(owner == holder)
        here, near, far = owners
        alive = [jnp.broadcast_to((cnt[...] > row).astype(jnp.float32), (SUB, LANES)) for row in (0, 1)]
        colours = jnp.broadcast_to(col[...], (SUB, LANES))
        coef = (c0, c1)

        def minus(begin, row, j, value, held_by, sign):
            for k in range(FACES):
                taken = jnp.take_along_axis(value, lanes[k], axis=1, mode="promise_in_bounds")
                term = coef[row][k, tile(j), :] * jnp.where(held_by[k], taken, 0.0)
                begin = begin + term if sign > 0 else begin - term
            return begin

        def own_part(total, given, row, field):
            def body(j, _):
                total[tile(j), :] = minus(given[tile(j), :], row, j, field[tile(j), :], here, -1)
                return 0

            lax.fori_loop(0, TILES, body, 0, unroll=TILES)

        def take(total, buf, recv, side, kind, held_by, row, sign, scale=None):
            arrived(buf, recv, side, kind)

            def body(j, _):
                value = minus(total[tile(j), :], row, j, buf[side, kind, tile(j), :], held_by, sign)
                total[tile(j), :] = value if scale is None else scale * value
                return 0

            lax.fori_loop(0, TILES, body, 0, unroll=TILES)

        def solve_first(after_y, finish):
            y0 = f0.at[0]
            take(f1, h1, q1, quick, 1, near, 1, -1)
            take(y0, h1, q1, quick, 0, near, 0, -1)
            take(y0, h1, q1, slow, 0, far, 0, -1, alive[0])
            after_y()
            arrived(h1, q1, slow, 1)

            def forward(j, t):
                source = minus(f1[tile(j), :], 1, j, h1[slow, 1, tile(j), :], far, -1)
                f1[tile(j), :] = alive[1] * (source - t)

            products([(mat_l, y0)], forward, masks)
            products([(mat_p1, f1)], finish, masks)

        def solve_second(finish):
            y0 = f0.at[1]
            for side, held_by in ((quick, near), (slow, far)):
                take(f1, h2, q2, side, 2, held_by, 1, -1)
                take(y0, h2, q2, side, 1, held_by, 0, 1)
                take(y0, h2, q2, side, 0, held_by, 0, -1, alive[0] if held_by is far else None)

            def forward(j, t):
                f1[tile(j), :] = alive[1] * (f1[tile(j), :] - t)

            products([(mat_l, y0)], forward, masks)
            products([(mat_p1, f1)], finish, masks)

        return own_part, solve_first, solve_second, alive, colours

    @pl.when(w == 0)
    def _():
        mine = [local(prev.at[0], v0, 0), local(rhs.at[0], r0, 1), local(coupling.at[:, 0], c0, 2),
                local(neighbours, nb, 3), local(counts, cnt, 4), local(colour, col, 5),
                local(pivot.at[0], mat_p0, 6), local(upper.at[0], mat_u, 7)]
        pl.semaphore_wait(barrier, 3)

        @pl.when(s == 0)
        def _():
            start[0].start()

        first = [first_copy(side, 0) for side in (0, 1)]
        send_prev(0, first)
        for c in down:
            c.start()
        for c in mine:
            c.start()
        for c in mine:
            c.wait()
        own_part, solve_first, solve_second, alive, colours = make_solver()

        def term(j, t):
            part_t[tile(j), :] = jnp.where(colours == 0, alive[0] * t, v0[tile(j), :])

        def first0(j, t):
            cur0[tile(j), :] = part_t[tile(j), :] - jnp.where(colours == 0, alive[0] * t, 0.0)

        def second1(j, t):
            x1[tile(j), :] = alive[1] * t

        def second0(j, t):
            out[0, tile(j), :] = jnp.where(colours == 1, alive[0] * t, cur0[tile(j), :])

        up_y.wait_recv()
        products([(mat_p0, got_y)], term, masks)
        again = [again_copies(part_t, 0, core) for core in (1, 0)]
        start_slow_first(again[0])
        down_t.start()
        start_slow_first(again[1])
        up_x.wait_recv()
        products([(mat_u, got_x)], first0, masks)
        up[0].wait_recv()
        up[1].wait_recv()
        own_part(f0.at[1], r0, 0, cur0)
        up_cur.wait_recv()
        own_part(f1, r1, 1, cur1)
        up[2].wait_recv()
        up[3].wait_recv()
        solve_second(second1)
        products([(mat_p0, f0.at[1]), (mat_u, x1)], second0, masks)
        finish_sends(first, again[0] + again[1] + down + [down_t])

        @pl.when(s == 0)
        def _():
            start[0].wait_send()


    @pl.when(w == 1)
    def _():
        def greet(to, core):
            signal(barrier, to, core)

        greet(s, 0)
        greet(left, 0)
        greet(left, 1)

        @pl.when(s != last_line)
        def _():
            greet(right, 0)

        @pl.when(s < last_line - 1)
        def _():
            greet(right, 1)

        @pl.when(s == step1)
        def _():
            greet(0, 0)
            greet(0, 1)
            greet(step2, 1)

        @pl.when(s == step2)
        def _():
            greet(last_line, 1)

        mine = [local(prev.at[0], v1, 0), local(rhs.at[0], r1, 1), local(coupling.at[:, 0], c1, 2),
                local(neighbours, nb, 3), local(counts, cnt, 4), local(colour, col, 5),
                local(lower.at[0], mat_l, 6), local(pivot.at[0], mat_p1, 7)]
        ends = (s == 0) | (s == last_line)
        pl.semaphore_wait(barrier, jnp.where(ends, 1, 2) + jnp.where(ends | (s == step2), 1, 0))

        @pl.when(s == last_line)
        def _():
            signal(ready.at[0], step2, 1)

        @pl.when(s == step2)
        def _():
            signal(ready.at[0], step1, 1)

        @pl.when(s == last_line - 1)
        def _():
            signal(ready.at[1], last_line, 1)

        @pl.when(s == 0)
        def _():
            start[1].start()

        first = [first_copy(side, 1) for side in (0, 1)]
        send_prev(1, first)
        for c in mine:
            c.start()

        @pl.when(s == last_line)
        def _():
            pl.semaphore_wait(ready.at[1], 1)
            first[1].start()

        def pass_on(arriving, leaving):
            pl.semaphore_wait(ready.at[0], 1)
            for row in (0, 1):
                arriving[row].wait_recv()
                leaving[row].start()

        @pl.when(s == step1)
        def _():
            pass_on(start, middle)

        @pl.when(s == step2)
        def _():
            pass_on(middle, end)

        for c in mine[:6]:
            c.wait()
        own_part, solve_first, solve_second, alive, colours = make_solver()
        own_part(f1, r1, 1, v1)
        for c in down[:3]:
            c.wait_recv()
        for c in up[:3]:
            c.start()
        own_part(f0.at[0], r0, 0, v0)
        mine[6].wait()
        mine[7].wait()

        def first1(j, t):
            x1[tile(j), :] = alive[1] * t
            cur1[tile(j), :] = jnp.where(colours == 0, alive[1] * t, v1[tile(j), :])

        def term(j, t):
            part_u[tile(j), :] = jnp.where(colours == 0, alive[0] * t, 0.0)

        def second1(j, t):
            out[0, tile(j), :] = jnp.where(colours == 1, alive[1] * t, cur1[tile(j), :])

        solve_first(up_y.start, first1)
        again1 = [again_copies(cur1, 2, core) for core in (1, 0)]
        start_slow_first(again1[0])
        down[3].wait_recv()
        products([(mat_u, x1)], term, masks)
        again0 = [again_copies(part_u, 1, core) for core in (1, 0)]
        start_slow_first(again0[0])
        up_x.start()
        up_cur.start()
        start_slow_first(again0[1])
        start_slow_first(again1[1])
        up[3].start()
        own_part(f1, r1, 1, cur1)
        down_t.wait_recv()

        def join(j, _):
            cur0[tile(j), :] = part_t[tile(j), :] - part_u[tile(j), :]
            return 0

        lax.fori_loop(0, TILES, join, 0, unroll=TILES)
        own_part(f0.at[1], r0, 0, cur0)
        solve_second(second1)
        finish_sends(first, up + [up_cur, up_y, up_x] + again0[0] + again0[1] + again1[0] + again1[1])

        @pl.when(s == 0)
        def _():
            start[1].wait_send()

        @pl.when(s == step1)
        def _():
            for c in middle:
                c.wait_send()

        @pl.when(s == step2)
        def _():
            for c in end:
                c.wait_send()


def shards(groups, rhs, prev_solution, lower, pivot_inv, upper_back, coupling, neighbours, counts, colour):
    plane = pltpu.VMEM((BLOCK, LANES), jnp.float32)
    matrix = pltpu.VMEM((BLOCK, BLOCK, LANES), jnp.float32)
    faces = pltpu.VMEM((FACES, BLOCK, LANES), jnp.float32)
    pair = pltpu.VMEM((2, BLOCK, LANES), jnp.float32)
    line = pltpu.VMEM((1, LANES), jnp.int32)
    dma = pltpu.SemaphoreType.DMA
    here = (rhs, prev_solution, lower, pivot_inv, upper_back, coupling, neighbours,
            counts.reshape(1, LANES), colour.reshape(1, LANES))
    return pl.pallas_call(
        functools.partial(kernel, groups),
        out_shape=pltpu.VMEM((1, BLOCK, LANES), jnp.float32),
        in_specs=[pl.BlockSpec(memory_space=pltpu.HBM)] * 9,
        out_specs=pl.BlockSpec(memory_space=pltpu.VMEM),
        scratch_shapes=[matrix] * 4 + [plane] * 4 + [faces] * 2
        + [pltpu.VMEM((FACES, LANES), jnp.int32), line, line]
        + [pltpu.VMEM((2, 2, BLOCK, LANES), jnp.float32), pltpu.VMEM((2, 3, BLOCK, LANES), jnp.float32), pair]
        + [plane] * 8 + [pair]
        + [dma((8,)), dma((12,)), dma((12,)), dma((2,)), dma((2, 2)), dma((3, 2, 2)), dma((2, 3)), dma((2,)), dma((2,))]
        + [pltpu.SemaphoreType.REGULAR((2,))],
        compiler_params=pltpu.CompilerParams(collective_id=0, has_side_effects=True, vmem_limit_bytes=16 << 20),
    )(*[pltpu.with_memory_space_constraint(a, pltpu.HBM) for a in here])


def solution(mesh):
    placed = (
        P("wall", None, "surf"),
        P("wall", None, "surf"),
        P("wall", None, None, "surf"),
        P("wall", None, None, "surf"),
        P("wall", None, None, "surf"),
        P(None, "wall", None, "surf"),
        P(None, "surf"),
        P("surf"),
        P("surf"),
    )
    return jax.shard_map(
        functools.partial(shards, mesh.shape["surf"]), mesh=mesh, in_specs=placed, out_specs=P("wall", None, "surf"),
        check_vma=False,
    )
```

```python
import functools

import jax
import jax.numpy as jnp
from jax import lax
from jax.experimental import pallas as pl
from jax.experimental.pallas import tpu as pltpu
from jax.sharding import PartitionSpec as P

MESH = pl.DeviceIdType.MESH
BLOCK = 64
FACES = 4
LANES = 128
SUB = 8
TILES = BLOCK // SUB
HALVES = {0: pl.ds(0, BLOCK // 2), 3: pl.ds(BLOCK // 2, BLOCK // 2)}
ROW = 4
PLANE = 16


def tile(j):
    return pl.ds(pl.multiple_of(j * SUB, SUB), SUB)


def fold(parts, masks):
    step = 1
    for mask in masks:
        merged = []
        for base in range(0, len(parts), 2):
            a, b = parts[base], parts[base + 1]
            merged.append(jnp.where(mask, a, b) + pltpu.roll(jnp.where(mask, b, a), step, 0))
        parts = merged
        step *= 2
    return parts[0]


def tree(terms):
    while len(terms) > 1:
        terms = [terms[i] + terms[i + 1] for i in range(0, len(terms) - 1, 2)] + terms[len(terms) & ~1:]
    return terms[0]


def products(pairs, finish, masks, first=0, last=TILES):
    vecs = [[vec[pl.ds(SUB * b, SUB), :] for b in range(TILES)] for _, vec in pairs]

    def body(j, _):
        parts = []
        for a in range(SUB):
            row = j * SUB + a
            terms = []
            for (mat, _), vec in zip(pairs, vecs):
                terms.append(tree([mat[row, pl.ds(SUB * b, SUB), :] * vec[b] for b in range(TILES)]))
            parts.append(terms[0] if len(terms) == 1 else terms[0] - terms[1])
        finish(j, fold(parts, masks))
        return 0

    lax.fori_loop(first, last, body, 0, unroll=last - first)


def kernel(groups, rhs, prev, lower, pivot, upper, coupling, neighbours, counts, colour, out,
           mat_l, mat_p1, mat_p0, mat_u, v0, v1, r0, r1, c0, c1, nb, cnt, col, h1, h2, f0, f1, x1, cur0, cur1, part_t, part_u, early,
           got_y, got_x, hop, loc, wsend, wrecv, s1, q1, s2, q2, rsend, rrecv, ready):
    s = lax.axis_index("surf")
    w = lax.axis_index("wall")
    right = lax.rem(s + 1, groups)
    left = lax.rem(s + groups - 1, groups)
    place = lax.rem(s, ROW)
    last_line = groups - 1
    sub = lax.broadcasted_iota(jnp.int32, (SUB, LANES), 0)
    masks = [(sub & 1) == 0, (sub & 2) == 0, (sub & 4) == 0]
    barrier = pltpu.get_barrier_semaphore()
    slow = jnp.where(place == ROW - 1, 1, 0)
    quick = 1 - slow
    slow_line = jnp.where(slow == 1, right, left)
    quick_line = jnp.where(slow == 1, left, right)

    def signal(sem, to, core):
        pl.semaphore_signal(sem, inc=1, device_id=(to, core), device_id_type=MESH)

    def local(src, dst, i):
        return pltpu.make_async_copy(src, dst, loc.at[i])

    def wall_copy(src, dst, i, to):
        return pltpu.make_async_remote_copy(src_ref=src, dst_ref=dst, send_sem=wsend.at[i], recv_sem=wrecv.at[i],
                                            device_id=(s, to), device_id_type=MESH)

    def first_copy(side, row):
        return pltpu.make_async_remote_copy(
            src_ref=prev.at[0], dst_ref=h1.at[side, row], send_sem=s1.at[side], recv_sem=q1.at[side, row],
            device_id=(right if side == 0 else left, 1), device_id_type=MESH)

    def again_copy(src, kind, side, core):
        dst = h2.at[side, kind % 3]
        if kind in HALVES:
            src, dst = src.at[HALVES[kind]], dst.at[HALVES[kind]]
        return pltpu.make_async_remote_copy(
            src_ref=src, dst_ref=dst, send_sem=s2.at[kind, side, core], recv_sem=q2.at[side, kind],
            device_id=(right if side == 0 else left, core), device_id_type=MESH)

    def again_copies(src, kind):
        return [again_copy(src, kind, side, 1) for side in (0, 1)]

    def twin(src, kind, act):
        for source, side in ((last_line, 0), (1, 1)):
            @pl.when(s == source)
            def _():
                act(again_copy(src, kind, side, 0))

    down = [wall_copy(prev.at[0], v0, 0, 1), wall_copy(rhs.at[0], r0, 1, 1), wall_copy(coupling.at[:, 0], c0, 2, 1),
            wall_copy(upper.at[0], mat_u, 3, 1)]
    down_t = wall_copy(part_t, part_t, 4, 1)
    up = [wall_copy(rhs.at[0], r1, 5, 0), wall_copy(coupling.at[:, 0], c1, 6, 0), wall_copy(lower.at[0], mat_l, 7, 0),
          wall_copy(pivot.at[0], mat_p1, 8, 0)]
    up_cur = wall_copy(cur1, cur1, 9, 0)
    up_early = wall_copy(early, got_y.at[0], 10, 0)
    up_y = [wall_copy(f0.at[i], got_y.at[i], 10 + i, 0) for i in (0, 1)]
    up_x = [wall_copy(x1.at[i], got_x.at[i], 12 + i, 0) for i in (0, 1)]

    def start_slow_first(copies):
        @pl.when(place == 0)
        def _():
            copies[1].start()
            copies[0].start()

        @pl.when(place != 0)
        def _():
            copies[0].start()
            copies[1].start()

    def send_prev(row, copies):
        copies[0].start()

        @pl.when((s != 0) & (s != last_line))
        def _():
            copies[1].start()

    def send_prev_late(copies):
        pl.semaphore_wait(ready.at[1], 1)
        copies[1].start()

    step1, step2 = ROW - 1, PLANE - 1

    def relay(src, dst, row, to, recv):
        return pltpu.make_async_remote_copy(
            src_ref=src, dst_ref=dst, send_sem=rsend.at[row], recv_sem=recv, device_id=(to, 1), device_id_type=MESH)

    start = [relay(prev.at[0], hop.at[row], row, step1, rrecv.at[row]) for row in (0, 1)]
    middle = [relay(hop.at[row], hop.at[row], row, step2, rrecv.at[row]) for row in (0, 1)]
    end = [relay(hop.at[row], h1.at[1, row], row, last_line, q1.at[1, row]) for row in (0, 1)]
    end_twin = pltpu.make_async_remote_copy(
        src_ref=hop.at[0], dst_ref=h1.at[1, 0], send_sem=rsend.at[2], recv_sem=q1.at[1, 0], device_id=(last_line, 0),
        device_id_type=MESH)

    def finish_sends(first, others):
        for c in [first[0]] + others:
            c.wait_send()

        @pl.when(s != 0)
        def _():
            first[1].wait_send()

    def arrived(buf, recv, side, kind, half=None):
        ref = buf.at[side, kind % 3]
        if half is not None:
            ref = ref.at[half]
        pltpu.make_async_copy(ref, ref, recv.at[side, kind]).wait()

    def make_solver():
        owners = ([], [], [])
        lanes = []
        for k in range(FACES):
            line = nb[pl.ds(k, 1), :]
            lanes.append(jnp.broadcast_to(line & (LANES - 1), (SUB, LANES)))
            owner = jnp.broadcast_to(line >> 7, (SUB, LANES))
            for masks_of, holder in zip(owners, (s, quick_line, slow_line)):
                masks_of.append(owner == holder)
        here, near, far = owners
        alive = [jnp.broadcast_to((cnt[...] > row).astype(jnp.float32), (SUB, LANES)) for row in (0, 1)]
        colours = jnp.broadcast_to(col[...], (SUB, LANES))
        coef = (c0, c1)

        def minus(begin, row, j, value, held_by, sign):
            for k in range(FACES):
                taken = jnp.take_along_axis(value, lanes[k], axis=1, mode="promise_in_bounds")
                term = coef[row][k, tile(j), :] * jnp.where(held_by[k], taken, 0.0)
                begin = begin + term if sign > 0 else begin - term
            return begin

        def own_part(total, given, row, field):
            def body(j, _):
                total[tile(j), :] = minus(given[tile(j), :], row, j, field[tile(j), :], here, -1)
                return 0

            lax.fori_loop(0, TILES, body, 0, unroll=TILES)

        def take(total, buf, recv, side, kind, held_by, row, sign, scale=None, half=None):
            arrived(buf, recv, side, kind, half)

            def body(j, _):
                value = minus(total[tile(j), :], row, j, buf[side, kind % 3, tile(j), :], held_by, sign)
                total[tile(j), :] = value if scale is None else scale * value
                return 0

            begin = 0 if half is None else half.start // SUB
            count = TILES if half is None else half.size // SUB
            lax.fori_loop(begin, begin + count, body, 0, unroll=count)

        def far_first(total):
            take(total, h1, q1, slow, 0, far, 0, -1, alive[0])

        def solve_first(finish):
            y0 = f0.at[0]
            take(y0, h1, q1, quick, 0, near, 0, -1)

            @pl.when(s == last_line)
            def _():
                early[...] = y0[...]
                up_early.start()

            take(f1, h1, q1, quick, 1, near, 1, -1)
            far_first(y0)

            @pl.when(s != last_line)
            def _():
                up_y[0].start()

            arrived(h1, q1, slow, 1)

            def forward(j, t):
                source = minus(f1[tile(j), :], 1, j, h1[slow, 1, tile(j), :], far, -1)
                f1[tile(j), :] = alive[1] * (source - t)

            products([(mat_l, y0)], forward, masks)
            products([(mat_p1, f1)], finish, masks)

        def solve_second(after_y, finish):
            y0 = f0.at[1]
            for side, held_by in ((quick, near), (slow, far)):
                take(f1, h2, q2, side, 2, held_by, 1, -1)
                take(y0, h2, q2, side, 1, held_by, 0, 1)
                for kind, half in HALVES.items():
                    take(y0, h2, q2, side, kind, held_by, 0, -1, alive[0] if held_by is far else None, half)
            after_y()

            def forward(j, t):
                f1[tile(j), :] = alive[1] * (f1[tile(j), :] - t)

            products([(mat_l, y0)], forward, masks)
            products([(mat_p1, f1)], finish, masks)

        return own_part, far_first, solve_first, solve_second, alive, colours

    @pl.when(w == 0)
    def _():
        mine = [local(prev.at[0], v0, 0), local(rhs.at[0], r0, 1), local(coupling.at[:, 0], c0, 2),
                local(neighbours, nb, 3), local(counts, cnt, 4), local(colour, col, 5),
                local(pivot.at[0], mat_p0, 6), local(upper.at[0], mat_u, 7)]
        pl.semaphore_wait(barrier, 3)

        @pl.when(s == 0)
        def _():
            start[0].start()

        @pl.when(s == last_line)
        def _():
            signal(ready.at[2], step2, 1)

        first = [first_copy(side, 0) for side in (0, 1)]
        send_prev(0, first)
        for c in down:
            c.start()
        for c in mine:
            c.start()

        @pl.when(s == last_line)
        def _():
            send_prev_late(first)

        for c in mine:
            c.wait()
        own_part, far_first, solve_first, solve_second, alive, colours = make_solver()

        def term(j, t):
            part_t[tile(j), :] = jnp.where(colours == 0, alive[0] * t, v0[tile(j), :])

        def first0(j, t):
            cur0[tile(j), :] = part_t[tile(j), :] - jnp.where(colours == 0, alive[0] * t, 0.0)

        def keep(j, t):
            part_u[tile(j), :] = t

        def result(j, t):
            out[0, tile(j), :] = jnp.where(colours == 1, alive[0] * t, cur0[tile(j), :])

        up_y[0].wait_recv()

        @pl.when(s == last_line)
        def _():
            far_first(got_y.at[0])

        again = []
        for kind, half in HALVES.items():
            begin = half.start // SUB
            products([(mat_p0, got_y.at[0])], term, masks, begin, begin + half.size // SUB)
            copies = again_copies(part_t, kind)
            start_slow_first(copies)
            again += copies
        down_t.start()
        for kind in HALVES:
            twin(part_t, kind, lambda c: c.start())
        up_x[0].wait_recv()
        products([(mat_u, got_x.at[0])], first0, masks)

        @pl.when(s == 0)
        def _():
            def second1(j, t):
                x1[1, tile(j), :] = alive[1] * t

            up[0].wait_recv()
            up[1].wait_recv()
            own_part(f0.at[1], r0, 0, cur0)
            up_cur.wait_recv()
            own_part(f1, r1, 1, cur1)
            up[2].wait_recv()
            up[3].wait_recv()
            solve_second(lambda: None, second1)
            products([(mat_p0, f0.at[1]), (mat_u, x1.at[1])], result, masks)
            start[0].wait_send()

        @pl.when(s != 0)
        def _():
            up_y[1].wait_recv()
            products([(mat_p0, got_y.at[1])], keep, masks)
            up_x[1].wait_recv()
            products([(mat_u, got_x.at[1])], lambda j, t: result(j, part_u[tile(j), :] - t), masks)

        for kind in HALVES:
            twin(part_t, kind, lambda c: c.wait_send())
        finish_sends(first, again + down + [down_t])

    @pl.when(w == 1)
    def _():
        def greet(to, core):
            signal(barrier, to, core)

        greet(s, 0)
        greet(left, 0)
        greet(left, 1)

        @pl.when(s < last_line - 1)
        def _():
            greet(right, 0)
            greet(right, 1)

        @pl.when(s == step1)
        def _():
            greet(0, 0)
            greet(0, 1)
            greet(step2, 1)

        @pl.when(s == step2)
        def _():
            greet(last_line, 0)
            greet(last_line, 1)

        mine = [local(prev.at[0], v1, 0), local(rhs.at[0], r1, 1), local(coupling.at[:, 0], c1, 2),
                local(neighbours, nb, 3), local(counts, cnt, 4), local(colour, col, 5),
                local(lower.at[0], mat_l, 6), local(pivot.at[0], mat_p1, 7)]
        ends = (s == 0) | (s == last_line)
        pl.semaphore_wait(barrier, jnp.where(ends, 1, 2) + jnp.where(ends | (s == step2), 1, 0))

        @pl.when(s == last_line)
        def _():
            signal(ready.at[0], step2, 1)

        @pl.when(s == step2)
        def _():
            signal(ready.at[0], step1, 1)

        @pl.when(s == last_line - 1)
        def _():
            signal(ready.at[1], last_line, 1)

        @pl.when(s == 0)
        def _():
            start[1].start()

        first = [first_copy(side, 1) for side in (0, 1)]
        send_prev(1, first)
        for c in mine:
            c.start()

        @pl.when(s == last_line)
        def _():
            send_prev_late(first)

        def pass_on(arriving, leaving):
            pl.semaphore_wait(ready.at[0], 1)
            for row in (0, 1):
                arriving[row].wait_recv()
                leaving[row].start()

        @pl.when(s == step1)
        def _():
            pass_on(start, middle)

        @pl.when(s == step2)
        def _():
            pass_on(middle, end)
            pl.semaphore_wait(ready.at[2], 1)
            end_twin.start()

        for c in mine[:6]:
            c.wait()
        own_part, far_first, solve_first, solve_second, alive, colours = make_solver()
        own_part(f1, r1, 1, v1)
        for c in down[:3]:
            c.wait_recv()

        @pl.when(s == last_line)
        def _():
            signal(ready.at[1], last_line, 0)

        @pl.when(s == 0)
        def _():
            for c in up:
                c.start()

        own_part(f0.at[0], r0, 0, v0)
        mine[6].wait()
        mine[7].wait()

        def first1(j, t):
            x1[0, tile(j), :] = alive[1] * t
            cur1[tile(j), :] = jnp.where(colours == 0, alive[1] * t, v1[tile(j), :])

        def term(j, t):
            part_u[tile(j), :] = jnp.where(colours == 0, alive[0] * t, 0.0)

        def second1(j, t):
            x1[1, tile(j), :] = alive[1] * t
            out[0, tile(j), :] = jnp.where(colours == 1, alive[1] * t, cur1[tile(j), :])

        solve_first(first1)
        again1 = again_copies(cur1, 2)
        start_slow_first(again1)
        down[3].wait_recv()
        products([(mat_u, x1.at[0])], term, masks)
        again0 = again_copies(part_u, 1)
        start_slow_first(again0)
        up_x[0].start()
        own_part(f1, r1, 1, cur1)
        down_t.wait_recv()
        twin(cur1, 2, lambda c: c.start())
        twin(part_u, 1, lambda c: c.start())

        @pl.when(s == 0)
        def _():
            up_cur.start()

        def join(j, _):
            cur0[tile(j), :] = part_t[tile(j), :] - part_u[tile(j), :]
            return 0

        lax.fori_loop(0, TILES, join, 0, unroll=TILES)
        own_part(f0.at[1], r0, 0, cur0)

        def after_y():
            @pl.when(s != 0)
            def _():
                up_y[1].start()

        solve_second(after_y, second1)

        @pl.when(s != 0)
        def _():
            up_x[1].start()

        twin(cur1, 2, lambda c: c.wait_send())
        twin(part_u, 1, lambda c: c.wait_send())
        finish_sends(first, [up_y[0], up_x[0]] + again0 + again1)

        @pl.when(s != 0)
        def _():
            up_y[1].wait_send()
            up_x[1].wait_send()

        @pl.when(s == 0)
        def _():
            for c in up + [up_cur]:
                c.wait_send()

        @pl.when(s == 0)
        def _():
            start[1].wait_send()

        @pl.when(s == step1)
        def _():
            for c in middle:
                c.wait_send()

        @pl.when(s == step2)
        def _():
            for c in end + [end_twin]:
                c.wait_send()


def shards(groups, rhs, prev_solution, lower, pivot_inv, upper_back, coupling, neighbours, counts, colour):
    plane = pltpu.VMEM((BLOCK, LANES), jnp.float32)
    matrix = pltpu.VMEM((BLOCK, BLOCK, LANES), jnp.float32)
    faces = pltpu.VMEM((FACES, BLOCK, LANES), jnp.float32)
    pair = pltpu.VMEM((2, BLOCK, LANES), jnp.float32)
    line = pltpu.VMEM((1, LANES), jnp.int32)
    dma = pltpu.SemaphoreType.DMA
    here = (rhs, prev_solution, lower, pivot_inv, upper_back, coupling, neighbours,
            counts.reshape(1, LANES), colour.reshape(1, LANES))
    return pl.pallas_call(
        functools.partial(kernel, groups),
        out_shape=pltpu.VMEM((1, BLOCK, LANES), jnp.float32),
        in_specs=[pl.BlockSpec(memory_space=pltpu.HBM)] * 9,
        out_specs=pl.BlockSpec(memory_space=pltpu.VMEM),
        scratch_shapes=[matrix] * 4 + [plane] * 4 + [faces] * 2
        + [pltpu.VMEM((FACES, LANES), jnp.int32), line, line]
        + [pltpu.VMEM((2, 2, BLOCK, LANES), jnp.float32), pltpu.VMEM((2, 3, BLOCK, LANES), jnp.float32), pair]
        + [plane, pair] + [plane] * 5 + [pair] * 3
        + [dma((8,)), dma((14,)), dma((14,)), dma((2,)), dma((2, 2)), dma((4, 2, 2)), dma((2, 4)), dma((3,)), dma((2,))]
        + [pltpu.SemaphoreType.REGULAR((3,))],
        compiler_params=pltpu.CompilerParams(collective_id=0, has_side_effects=True, vmem_limit_bytes=16 << 20),
    )(*[pltpu.with_memory_space_constraint(a, pltpu.HBM) for a in here])


def solution(mesh):
    placed = (
        P("wall", None, "surf"),
        P("wall", None, "surf"),
        P("wall", None, None, "surf"),
        P("wall", None, None, "surf"),
        P("wall", None, None, "surf"),
        P(None, "wall", None, "surf"),
        P(None, "surf"),
        P("surf"),
        P("surf"),
    )
    return jax.shard_map(
        functools.partial(shards, mesh.shape["surf"]), mesh=mesh, in_specs=placed, out_specs=P("wall", None, "surf"),
        check_vma=False,
    )
```

```python
import functools

import jax
import jax.numpy as jnp
from jax import lax
from jax.experimental import pallas as pl
from jax.experimental.pallas import tpu as pltpu
from jax.sharding import PartitionSpec as P

MESH = pl.DeviceIdType.MESH
BLOCK = 64
FACES = 4
LANES = 128
SUB = 8
TILES = BLOCK // SUB
HALVES = {0: pl.ds(0, BLOCK // 2), 3: pl.ds(BLOCK // 2, BLOCK // 2)}
ROW = 4
PLANE = 16


def tile(j):
    return pl.ds(pl.multiple_of(j * SUB, SUB), SUB)


def fold(parts, masks):
    step = 1
    for mask in masks:
        merged = []
        for base in range(0, len(parts), 2):
            a, b = parts[base], parts[base + 1]
            merged.append(jnp.where(mask, a, b) + pltpu.roll(jnp.where(mask, b, a), step, 0))
        parts = merged
        step *= 2
    return parts[0]


def tree(terms):
    while len(terms) > 1:
        terms = [terms[i] + terms[i + 1] for i in range(0, len(terms) - 1, 2)] + terms[len(terms) & ~1:]
    return terms[0]


def products(pairs, finish, masks, first=0, last=TILES):
    vecs = [[vec[pl.ds(SUB * b, SUB), :] for b in range(TILES)] for _, vec in pairs]

    def body(j, _):
        parts = []
        for a in range(SUB):
            row = j * SUB + a
            terms = []
            for (mat, _), vec in zip(pairs, vecs):
                terms.append(tree([mat[row, pl.ds(SUB * b, SUB), :] * vec[b] for b in range(TILES)]))
            parts.append(terms[0] if len(terms) == 1 else terms[0] - terms[1])
        finish(j, fold(parts, masks))
        return 0

    lax.fori_loop(first, last, body, 0, unroll=last - first)


def kernel(groups, rhs, prev, lower, pivot, upper, coupling, neighbours, counts, colour, out,
           mat_l, mat_p1, mat_p0, mat_u, v0, v1, r0, r1, c0, c1, nb, cnt, col, h1, h2, f0, f1, x1, cur0, cur1, part_t, part_u, early,
           got_y, got_x, hop, loc, wsend, wrecv, s1, q1, s2, q2, rsend, rrecv, ready):
    s = lax.axis_index("surf")
    w = lax.axis_index("wall")
    right = lax.rem(s + 1, groups)
    left = lax.rem(s + groups - 1, groups)
    place = lax.rem(s, ROW)
    last_line = groups - 1
    sub = lax.broadcasted_iota(jnp.int32, (SUB, LANES), 0)
    masks = [(sub & 1) == 0, (sub & 2) == 0, (sub & 4) == 0]
    barrier = pltpu.get_barrier_semaphore()
    slow = jnp.where(place == ROW - 1, 1, 0)
    quick = 1 - slow
    slow_line = jnp.where(slow == 1, right, left)
    quick_line = jnp.where(slow == 1, left, right)

    def signal(sem, to, core):
        pl.semaphore_signal(sem, inc=1, device_id=(to, core), device_id_type=MESH)

    def local(src, dst, i):
        return pltpu.make_async_copy(src, dst, loc.at[i])

    def wall_copy(src, dst, i, to):
        return pltpu.make_async_remote_copy(src_ref=src, dst_ref=dst, send_sem=wsend.at[i], recv_sem=wrecv.at[i],
                                            device_id=(s, to), device_id_type=MESH)

    def first_copy(side, row):
        return pltpu.make_async_remote_copy(
            src_ref=prev.at[0], dst_ref=h1.at[side, row], send_sem=s1.at[side], recv_sem=q1.at[side, row],
            device_id=(right if side == 0 else left, 1), device_id_type=MESH)

    def again_copy(src, kind, side, core):
        dst = h2.at[side, kind % 3]
        if kind in HALVES:
            src, dst = src.at[HALVES[kind]], dst.at[HALVES[kind]]
        return pltpu.make_async_remote_copy(
            src_ref=src, dst_ref=dst, send_sem=s2.at[kind, side, core], recv_sem=q2.at[side, kind],
            device_id=(right if side == 0 else left, core), device_id_type=MESH)

    def again_copies(src, kind):
        return [again_copy(src, kind, side, 1) for side in (0, 1)]

    def twin(src, kind, act):
        for source, side in ((last_line, 0), (1, 1)):
            @pl.when(s == source)
            def _():
                act(again_copy(src, kind, side, 0))

    down = [wall_copy(prev.at[0], v0, 0, 1), wall_copy(rhs.at[0], r0, 1, 1), wall_copy(coupling.at[:, 0], c0, 2, 1),
            wall_copy(upper.at[0], mat_u, 3, 1)]
    down_t = wall_copy(part_t, part_t, 4, 1)
    up = [wall_copy(rhs.at[0], r1, 5, 0), wall_copy(coupling.at[:, 0], c1, 6, 0), wall_copy(lower.at[0], mat_l, 7, 0),
          wall_copy(pivot.at[0], mat_p1, 8, 0)]
    up_cur = wall_copy(cur1, cur1, 9, 0)
    up_early = wall_copy(early, got_y.at[0], 10, 0)
    up_y = wall_copy(f0.at[1], got_y.at[1], 11, 0)
    up_far = pltpu.make_async_remote_copy(
        src_ref=h1.at[slow, 0], dst_ref=h1.at[slow, 0], send_sem=wsend.at[14], recv_sem=q1.at[slow, 0], device_id=(s, 0),
        device_id_type=MESH)
    up_x = [wall_copy(x1.at[i], got_x.at[i], 12 + i, 0) for i in (0, 1)]

    def start_slow_first(copies):
        @pl.when(place == 0)
        def _():
            copies[1].start()
            copies[0].start()

        @pl.when(place != 0)
        def _():
            copies[0].start()
            copies[1].start()

    def send_prev(row, copies):
        copies[0].start()

        @pl.when((s != 0) & (s != last_line))
        def _():
            copies[1].start()

    def send_prev_late(copies):
        pl.semaphore_wait(ready.at[1], 1)
        copies[1].start()

    step1, step2 = ROW - 1, PLANE - 1

    def relay(src, dst, row, to, recv):
        return pltpu.make_async_remote_copy(
            src_ref=src, dst_ref=dst, send_sem=rsend.at[row], recv_sem=recv, device_id=(to, 1), device_id_type=MESH)

    start = [relay(prev.at[0], hop.at[row], row, step1, rrecv.at[row]) for row in (0, 1)]
    middle = [relay(hop.at[row], hop.at[row], row, step2, rrecv.at[row]) for row in (0, 1)]
    end = [relay(hop.at[row], h1.at[1, row], row, last_line, q1.at[1, row]) for row in (0, 1)]

    def finish_sends(first, others):
        for c in [first[0]] + others:
            c.wait_send()

        @pl.when(s != 0)
        def _():
            first[1].wait_send()

    def arrived(buf, recv, side, kind, half=None):
        ref = buf.at[side, kind % 3]
        if half is not None:
            ref = ref.at[half]
        pltpu.make_async_copy(ref, ref, recv.at[side, kind]).wait()

    def make_solver():
        owners = ([], [], [])
        lanes = []
        for k in range(FACES):
            line = nb[pl.ds(k, 1), :]
            lanes.append(jnp.broadcast_to(line & (LANES - 1), (SUB, LANES)))
            owner = jnp.broadcast_to(line >> 7, (SUB, LANES))
            for masks_of, holder in zip(owners, (s, quick_line, slow_line)):
                masks_of.append(owner == holder)
        here, near, far = owners
        alive = [jnp.broadcast_to((cnt[...] > row).astype(jnp.float32), (SUB, LANES)) for row in (0, 1)]
        colours = jnp.broadcast_to(col[...], (SUB, LANES))
        coef = (c0, c1)

        def minus(begin, row, j, value, held_by, sign):
            for k in range(FACES):
                taken = jnp.take_along_axis(value, lanes[k], axis=1, mode="promise_in_bounds")
                term = coef[row][k, tile(j), :] * jnp.where(held_by[k], taken, 0.0)
                begin = begin + term if sign > 0 else begin - term
            return begin

        def own_part(total, given, row, field):
            def body(j, _):
                total[tile(j), :] = minus(given[tile(j), :], row, j, field[tile(j), :], here, -1)
                return 0

            lax.fori_loop(0, TILES, body, 0, unroll=TILES)

        def take(total, buf, recv, side, kind, held_by, row, sign, scale=None, half=None):
            arrived(buf, recv, side, kind, half)

            def body(j, _):
                value = minus(total[tile(j), :], row, j, buf[side, kind % 3, tile(j), :], held_by, sign)
                total[tile(j), :] = value if scale is None else scale * value
                return 0

            begin = 0 if half is None else half.start // SUB
            count = TILES if half is None else half.size // SUB
            lax.fori_loop(begin, begin + count, body, 0, unroll=count)

        def far_first(total):
            def body(j, _):
                total[tile(j), :] = alive[0] * minus(total[tile(j), :], 0, j, h1[slow, 0, tile(j), :], far, -1)
                return 0

            lax.fori_loop(0, TILES, body, 0, unroll=TILES)

        def solve_first(finish):
            y0 = f0.at[0]
            take(y0, h1, q1, quick, 0, near, 0, -1)
            early[...] = y0[...]
            up_early.start()
            take(f1, h1, q1, quick, 1, near, 1, -1)
            arrived(h1, q1, slow, 0)
            up_far.start()
            far_first(y0)
            arrived(h1, q1, slow, 1)

            def forward(j, t):
                source = minus(f1[tile(j), :], 1, j, h1[slow, 1, tile(j), :], far, -1)
                f1[tile(j), :] = alive[1] * (source - t)

            products([(mat_l, y0)], forward, masks)
            products([(mat_p1, f1)], finish, masks)

        def solve_second(after_y, finish):
            y0 = f0.at[1]
            for side, held_by in ((quick, near), (slow, far)):
                take(f1, h2, q2, side, 2, held_by, 1, -1)
                take(y0, h2, q2, side, 1, held_by, 0, 1)
                for kind, half in HALVES.items():
                    take(y0, h2, q2, side, kind, held_by, 0, -1, alive[0] if held_by is far else None, half)
            after_y()

            def forward(j, t):
                f1[tile(j), :] = alive[1] * (f1[tile(j), :] - t)

            products([(mat_l, y0)], forward, masks)
            products([(mat_p1, f1)], finish, masks)

        return own_part, far_first, solve_first, solve_second, alive, colours

    @pl.when(w == 0)
    def _():
        mine = [local(prev.at[0], v0, 0), local(rhs.at[0], r0, 1), local(coupling.at[:, 0], c0, 2),
                local(neighbours, nb, 3), local(counts, cnt, 4), local(colour, col, 5),
                local(pivot.at[0], mat_p0, 6), local(upper.at[0], mat_u, 7)]
        pl.semaphore_wait(barrier, jnp.where(s == last_line, 2, 3))

        @pl.when(s == 0)
        def _():
            start[0].start()

        first = [first_copy(side, 0) for side in (0, 1)]
        send_prev(0, first)
        for c in down:
            c.start()
        for c in mine:
            c.start()

        @pl.when(s == last_line)
        def _():
            send_prev_late(first)

        for c in mine:
            c.wait()
        own_part, far_first, solve_first, solve_second, alive, colours = make_solver()

        def term(j, t):
            part_t[tile(j), :] = jnp.where(colours == 0, alive[0] * t, v0[tile(j), :])

        def first0(j, t):
            cur0[tile(j), :] = part_t[tile(j), :] - jnp.where(colours == 0, alive[0] * t, 0.0)

        def keep(j, t):
            part_u[tile(j), :] = t

        def result(j, t):
            out[0, tile(j), :] = jnp.where(colours == 1, alive[0] * t, cur0[tile(j), :])

        up_early.wait_recv()
        arrived(h1, q1, slow, 0)
        far_first(got_y.at[0])
        again = []
        for kind, half in HALVES.items():
            begin = half.start // SUB
            products([(mat_p0, got_y.at[0])], term, masks, begin, begin + half.size // SUB)
            copies = again_copies(part_t, kind)
            start_slow_first(copies)
            again += copies
        down_t.start()
        for kind in HALVES:
            twin(part_t, kind, lambda c: c.start())
        up_x[0].wait_recv()
        products([(mat_u, got_x.at[0])], first0, masks)

        @pl.when(s == 0)
        def _():
            def second1(j, t):
                x1[1, tile(j), :] = alive[1] * t

            up[0].wait_recv()
            up[1].wait_recv()
            own_part(f0.at[1], r0, 0, cur0)
            up_cur.wait_recv()
            own_part(f1, r1, 1, cur1)
            up[2].wait_recv()
            up[3].wait_recv()
            solve_second(lambda: None, second1)
            products([(mat_p0, f0.at[1]), (mat_u, x1.at[1])], result, masks)
            start[0].wait_send()

        @pl.when(s != 0)
        def _():
            up_y.wait_recv()
            products([(mat_p0, got_y.at[1])], keep, masks)
            up_x[1].wait_recv()
            products([(mat_u, got_x.at[1])], lambda j, t: result(j, part_u[tile(j), :] - t), masks)

        for kind in HALVES:
            twin(part_t, kind, lambda c: c.wait_send())
        finish_sends(first, again + down + [down_t])

    @pl.when(w == 1)
    def _():
        def greet(to, core):
            signal(barrier, to, core)

        @pl.when(s == last_line)
        def _():
            pl.semaphore_wait(barrier, 2)
            signal(ready.at[0], step2, 1)

        greet(left, 0)
        greet(left, 1)
        greet(s, 0)

        @pl.when(s < last_line - 1)
        def _():
            greet(right, 0)
            greet(right, 1)

        @pl.when(s == step1)
        def _():
            greet(0, 0)
            greet(0, 1)
            greet(step2, 1)

        @pl.when(s == step2)
        def _():
            greet(last_line, 1)

        mine = [local(prev.at[0], v1, 0), local(rhs.at[0], r1, 1), local(coupling.at[:, 0], c1, 2),
                local(neighbours, nb, 3), local(counts, cnt, 4), local(colour, col, 5),
                local(lower.at[0], mat_l, 6), local(pivot.at[0], mat_p1, 7)]

        @pl.when(s != last_line)
        def _():
            pl.semaphore_wait(barrier, jnp.where(s == step2, 3, 2))

        @pl.when(s == step2)
        def _():
            signal(ready.at[0], step1, 1)

        @pl.when(s == last_line - 1)
        def _():
            signal(ready.at[1], last_line, 1)

        @pl.when(s == 0)
        def _():
            start[1].start()

        first = [first_copy(side, 1) for side in (0, 1)]
        send_prev(1, first)
        for c in mine:
            c.start()

        @pl.when(s == last_line)
        def _():
            send_prev_late(first)

        def pass_on(arriving, leaving):
            pl.semaphore_wait(ready.at[0], 1)
            for row in (0, 1):
                arriving[row].wait_recv()
                leaving[row].start()

        @pl.when(s == step1)
        def _():
            pass_on(start, middle)

        @pl.when(s == step2)
        def _():
            pass_on(middle, end)

        for c in mine[:6]:
            c.wait()
        own_part, far_first, solve_first, solve_second, alive, colours = make_solver()
        own_part(f1, r1, 1, v1)
        for c in down[:3]:
            c.wait_recv()

        @pl.when(s == last_line)
        def _():
            signal(ready.at[1], last_line, 0)

        @pl.when(s == 0)
        def _():
            for c in up:
                c.start()

        own_part(f0.at[0], r0, 0, v0)
        mine[6].wait()
        mine[7].wait()

        def first1(j, t):
            x1[0, tile(j), :] = alive[1] * t
            cur1[tile(j), :] = jnp.where(colours == 0, alive[1] * t, v1[tile(j), :])

        def term(j, t):
            part_u[tile(j), :] = jnp.where(colours == 0, alive[0] * t, 0.0)

        def second1(j, t):
            x1[1, tile(j), :] = alive[1] * t
            out[0, tile(j), :] = jnp.where(colours == 1, alive[1] * t, cur1[tile(j), :])

        solve_first(first1)
        again1 = again_copies(cur1, 2)
        start_slow_first(again1)
        down[3].wait_recv()
        products([(mat_u, x1.at[0])], term, masks)
        again0 = again_copies(part_u, 1)
        start_slow_first(again0)
        up_x[0].start()
        own_part(f1, r1, 1, cur1)
        down_t.wait_recv()
        twin(cur1, 2, lambda c: c.start())
        twin(part_u, 1, lambda c: c.start())

        @pl.when(s == 0)
        def _():
            up_cur.start()

        def join(j, _):
            cur0[tile(j), :] = part_t[tile(j), :] - part_u[tile(j), :]
            return 0

        lax.fori_loop(0, TILES, join, 0, unroll=TILES)
        own_part(f0.at[1], r0, 0, cur0)

        def after_y():
            @pl.when(s != 0)
            def _():
                up_y.start()

        solve_second(after_y, second1)

        @pl.when(s != 0)
        def _():
            up_x[1].start()

        twin(cur1, 2, lambda c: c.wait_send())
        twin(part_u, 1, lambda c: c.wait_send())
        finish_sends(first, [up_early, up_far, up_x[0]] + again0 + again1)

        @pl.when(s != 0)
        def _():
            up_y.wait_send()
            up_x[1].wait_send()

        @pl.when(s == 0)
        def _():
            for c in up + [up_cur]:
                c.wait_send()

        @pl.when(s == 0)
        def _():
            start[1].wait_send()

        @pl.when(s == step1)
        def _():
            for c in middle:
                c.wait_send()

        @pl.when(s == step2)
        def _():
            for c in end:
                c.wait_send()


def shards(groups, rhs, prev_solution, lower, pivot_inv, upper_back, coupling, neighbours, counts, colour):
    plane = pltpu.VMEM((BLOCK, LANES), jnp.float32)
    matrix = pltpu.VMEM((BLOCK, BLOCK, LANES), jnp.float32)
    faces = pltpu.VMEM((FACES, BLOCK, LANES), jnp.float32)
    pair = pltpu.VMEM((2, BLOCK, LANES), jnp.float32)
    line = pltpu.VMEM((1, LANES), jnp.int32)
    dma = pltpu.SemaphoreType.DMA
    here = (rhs, prev_solution, lower, pivot_inv, upper_back, coupling, neighbours,
            counts.reshape(1, LANES), colour.reshape(1, LANES))
    return pl.pallas_call(
        functools.partial(kernel, groups),
        out_shape=pltpu.VMEM((1, BLOCK, LANES), jnp.float32),
        in_specs=[pl.BlockSpec(memory_space=pltpu.HBM)] * 9,
        out_specs=pl.BlockSpec(memory_space=pltpu.VMEM),
        scratch_shapes=[matrix] * 4 + [plane] * 4 + [faces] * 2
        + [pltpu.VMEM((FACES, LANES), jnp.int32), line, line]
        + [pltpu.VMEM((2, 2, BLOCK, LANES), jnp.float32), pltpu.VMEM((2, 3, BLOCK, LANES), jnp.float32), pair]
        + [plane, pair] + [plane] * 5 + [pair] * 3
        + [dma((8,)), dma((15,)), dma((15,)), dma((2,)), dma((2, 2)), dma((4, 2, 2)), dma((2, 4)), dma((2,)), dma((2,))]
        + [pltpu.SemaphoreType.REGULAR((2,))],
        compiler_params=pltpu.CompilerParams(collective_id=0, has_side_effects=True, vmem_limit_bytes=16 << 20),
    )(*[pltpu.with_memory_space_constraint(a, pltpu.HBM) for a in here])


def solution(mesh):
    placed = (
        P("wall", None, "surf"),
        P("wall", None, "surf"),
        P("wall", None, None, "surf"),
        P("wall", None, None, "surf"),
        P("wall", None, None, "surf"),
        P(None, "wall", None, "surf"),
        P(None, "surf"),
        P("surf"),
        P("surf"),
    )
    return jax.shard_map(
        functools.partial(shards, mesh.shape["surf"]), mesh=mesh, in_specs=placed, out_specs=P("wall", None, "surf"),
        check_vma=False,
    )
```

```python
import functools

import jax
import jax.numpy as jnp
from jax import lax
from jax.experimental import pallas as pl
from jax.experimental.pallas import tpu as pltpu
from jax.sharding import PartitionSpec as P

MESH = pl.DeviceIdType.MESH
BLOCK = 64
FACES = 4
LANES = 128
SUB = 8
TILES = BLOCK // SUB
HALVES = {0: pl.ds(0, BLOCK // 2), 3: pl.ds(BLOCK // 2, BLOCK // 2)}
PARTS = {0: HALVES[0], 2: HALVES[3]}
ROW = 4
PLANE = 16


def tile(j):
    return pl.ds(pl.multiple_of(j * SUB, SUB), SUB)


def fold(parts, masks):
    step = 1
    for mask in masks:
        merged = []
        for base in range(0, len(parts), 2):
            a, b = parts[base], parts[base + 1]
            merged.append(jnp.where(mask, a, b) + pltpu.roll(jnp.where(mask, b, a), step, 0))
        parts = merged
        step *= 2
    return parts[0]


def tree(terms):
    while len(terms) > 1:
        terms = [terms[i] + terms[i + 1] for i in range(0, len(terms) - 1, 2)] + terms[len(terms) & ~1:]
    return terms[0]


def products(pairs, finish, masks, first=0, last=TILES):
    vecs = [[vec[pl.ds(SUB * b, SUB), :] for b in range(TILES)] for _, vec in pairs]

    def body(j, _):
        parts = []
        for a in range(SUB):
            row = j * SUB + a
            terms = []
            for (mat, _), vec in zip(pairs, vecs):
                terms.append(tree([mat[row, pl.ds(SUB * b, SUB), :] * vec[b] for b in range(TILES)]))
            parts.append(terms[0] if len(terms) == 1 else terms[0] - terms[1])
        finish(j, fold(parts, masks))
        return 0

    lax.fori_loop(first, last, body, 0, unroll=last - first)


def kernel(groups, rhs, prev, lower, pivot, upper, coupling, neighbours, counts, colour, out,
           mat_l, mat_p1, mat_p0, mat_u, v0, v1, r0, r1, c0, c1, nb, cnt, col, h1, h2, f0, f1, x1, cur0, cur1, part_t, part_u, early,
           got_y, got_x, hop, loc, wsend, wrecv, s1, q1, s2, q2, rsend, rrecv, ready):
    s = lax.axis_index("surf")
    w = lax.axis_index("wall")
    right = lax.rem(s + 1, groups)
    left = lax.rem(s + groups - 1, groups)
    place = lax.rem(s, ROW)
    last_line = groups - 1
    sub = lax.broadcasted_iota(jnp.int32, (SUB, LANES), 0)
    masks = [(sub & 1) == 0, (sub & 2) == 0, (sub & 4) == 0]
    barrier = pltpu.get_barrier_semaphore()
    slow = jnp.where(place == ROW - 1, 1, 0)
    quick = 1 - slow
    slow_line = jnp.where(slow == 1, right, left)
    quick_line = jnp.where(slow == 1, left, right)

    def signal(sem, to, core):
        pl.semaphore_signal(sem, inc=1, device_id=(to, core), device_id_type=MESH)

    def local(src, dst, i):
        return pltpu.make_async_copy(src, dst, loc.at[i])

    def wall_copy(src, dst, i, to):
        return pltpu.make_async_remote_copy(src_ref=src, dst_ref=dst, send_sem=wsend.at[i], recv_sem=wrecv.at[i],
                                            device_id=(s, to), device_id_type=MESH)

    def piece(ref, part):
        return ref if part == 1 else ref.at[PARTS[part]]

    def first_copies(side, parts):
        return [pltpu.make_async_remote_copy(
            src_ref=piece(prev.at[0], part), dst_ref=piece(h1.at[side, part % 2], part), send_sem=s1.at[side, part],
            recv_sem=q1.at[side, part], device_id=(right if side == 0 else left, 1), device_id_type=MESH) for part in parts]

    def again_copy(src, kind, side, core):
        dst = h2.at[side, kind % 3]
        if kind in HALVES:
            src, dst = src.at[HALVES[kind]], dst.at[HALVES[kind]]
        return pltpu.make_async_remote_copy(
            src_ref=src, dst_ref=dst, send_sem=s2.at[kind, side, core], recv_sem=q2.at[side, kind],
            device_id=(right if side == 0 else left, core), device_id_type=MESH)

    def again_copies(src, kind):
        return [again_copy(src, kind, side, 1) for side in (0, 1)]

    def twin(src, kind, act):
        for source, side in ((last_line, 0), (1, 1)):
            @pl.when(s == source)
            def _():
                act(again_copy(src, kind, side, 0))

    down = [wall_copy(prev.at[0], v0, 0, 1), wall_copy(rhs.at[0], r0, 1, 1), wall_copy(coupling.at[:, 0], c0, 2, 1),
            wall_copy(upper.at[0], mat_u, 3, 1)]
    down_t = wall_copy(part_t, part_t, 4, 1)
    up = [wall_copy(rhs.at[0], r1, 5, 0), wall_copy(coupling.at[:, 0], c1, 6, 0), wall_copy(lower.at[0], mat_l, 7, 0),
          wall_copy(pivot.at[0], mat_p1, 8, 0)]
    up_cur = wall_copy(cur1, cur1, 9, 0)
    up_early = wall_copy(early, got_y.at[0], 10, 0)
    up_y = wall_copy(f0.at[1], got_y.at[1], 11, 0)
    up_far = {part: pltpu.make_async_remote_copy(
        src_ref=piece(h1.at[slow, 0], part), dst_ref=piece(h1.at[slow, 0], part), send_sem=wsend.at[14 + part // 2],
        recv_sem=q1.at[slow, part], device_id=(s, 0), device_id_type=MESH) for part in PARTS}
    up_x = [wall_copy(x1.at[i], got_x.at[i], 12 + i, 0) for i in (0, 1)]

    def start_slow_first(copies):
        @pl.when(place == 0)
        def _():
            copies[1].start()
            copies[0].start()

        @pl.when(place != 0)
        def _():
            copies[0].start()
            copies[1].start()

    def start_all(copies):
        for c in copies:
            c.start()

    def send_prev(copies):
        start_all(copies[0])

        @pl.when((s != 0) & (s != last_line))
        def _():
            start_all(copies[1])

    def send_prev_late(copies):
        pl.semaphore_wait(ready.at[1], 1)
        start_all(copies[1])

    step1, step2 = ROW - 1, PLANE - 1

    def relay(src, dst, part, to, recv):
        return pltpu.make_async_remote_copy(
            src_ref=piece(src, part), dst_ref=piece(dst, part), send_sem=rsend.at[part], recv_sem=recv, device_id=(to, 1),
            device_id_type=MESH)

    order = (0, 2, 1)
    start = {part: relay(prev.at[0], hop.at[part % 2], part, step1, rrecv.at[part]) for part in order}
    middle = {part: relay(hop.at[part % 2], hop.at[part % 2], part, step2, rrecv.at[part]) for part in order}
    end = {part: relay(hop.at[part % 2], h1.at[1, part % 2], part, last_line, q1.at[1, part]) for part in order}

    def finish_sends(first, others):
        for c in first[0] + others:
            c.wait_send()

        @pl.when(s != 0)
        def _():
            for c in first[1]:
                c.wait_send()

    def landed(side, part):
        ref = piece(h1.at[side, part % 2], part)
        pltpu.make_async_copy(ref, ref, q1.at[side, part]).wait()

    def arrived(buf, recv, side, kind, half=None):
        ref = buf.at[side, kind % 3]
        if half is not None:
            ref = ref.at[half]
        pltpu.make_async_copy(ref, ref, recv.at[side, kind]).wait()

    def make_solver():
        owners = ([], [], [])
        lanes = []
        for k in range(FACES):
            line = nb[pl.ds(k, 1), :]
            lanes.append(jnp.broadcast_to(line & (LANES - 1), (SUB, LANES)))
            owner = jnp.broadcast_to(line >> 7, (SUB, LANES))
            for masks_of, holder in zip(owners, (s, quick_line, slow_line)):
                masks_of.append(owner == holder)
        here, near, far = owners
        alive = [jnp.broadcast_to((cnt[...] > row).astype(jnp.float32), (SUB, LANES)) for row in (0, 1)]
        colours = jnp.broadcast_to(col[...], (SUB, LANES))
        coef = (c0, c1)

        def minus(begin, row, j, value, held_by, sign):
            for k in range(FACES):
                taken = jnp.take_along_axis(value, lanes[k], axis=1, mode="promise_in_bounds")
                term = coef[row][k, tile(j), :] * jnp.where(held_by[k], taken, 0.0)
                begin = begin + term if sign > 0 else begin - term
            return begin

        def own_part(total, given, row, field):
            def body(j, _):
                total[tile(j), :] = minus(given[tile(j), :], row, j, field[tile(j), :], here, -1)
                return 0

            lax.fori_loop(0, TILES, body, 0, unroll=TILES)

        def take(total, buf, recv, side, kind, held_by, row, sign, scale=None, half=None):
            arrived(buf, recv, side, kind, half)

            def body(j, _):
                value = minus(total[tile(j), :], row, j, buf[side, kind % 3, tile(j), :], held_by, sign)
                total[tile(j), :] = value if scale is None else scale * value
                return 0

            begin = 0 if half is None else half.start // SUB
            count = TILES if half is None else half.size // SUB
            lax.fori_loop(begin, begin + count, body, 0, unroll=count)

        def take_first(total, side, held_by, part, scale=None):
            row = part % 2

            def body(j, _):
                value = minus(total[tile(j), :], row, j, h1[side, row, tile(j), :], held_by, -1)
                total[tile(j), :] = value if scale is None else scale * value
                return 0

            begin = 0 if part == 1 else PARTS[part].start // SUB
            count = TILES if part == 1 else PARTS[part].size // SUB
            lax.fori_loop(begin, begin + count, body, 0, unroll=count)

        def far_first(total, part):
            take_first(total, slow, far, part, alive[0])

        def solve_first(finish):
            y0 = f0.at[0]
            for part in PARTS:
                landed(quick, part)
                take_first(y0, quick, near, part)
            early[...] = y0[...]
            up_early.start()
            landed(quick, 1)
            take_first(f1, quick, near, 1)
            for part in PARTS:
                landed(slow, part)
                up_far[part].start()
                far_first(y0, part)
            landed(slow, 1)

            def forward(j, t):
                source = minus(f1[tile(j), :], 1, j, h1[slow, 1, tile(j), :], far, -1)
                f1[tile(j), :] = alive[1] * (source - t)

            products([(mat_l, y0)], forward, masks)
            products([(mat_p1, f1)], finish, masks)

        def solve_second(after_y, finish):
            y0 = f0.at[1]
            for side, held_by in ((quick, near), (slow, far)):
                take(f1, h2, q2, side, 2, held_by, 1, -1)
                take(y0, h2, q2, side, 1, held_by, 0, 1)
                for kind, half in HALVES.items():
                    take(y0, h2, q2, side, kind, held_by, 0, -1, alive[0] if held_by is far else None, half)
            after_y()

            def forward(j, t):
                f1[tile(j), :] = alive[1] * (f1[tile(j), :] - t)

            products([(mat_l, y0)], forward, masks)
            products([(mat_p1, f1)], finish, masks)

        return own_part, far_first, solve_first, solve_second, alive, colours

    @pl.when(w == 0)
    def _():
        mine = [local(prev.at[0], v0, 0), local(rhs.at[0], r0, 1), local(coupling.at[:, 0], c0, 2),
                local(neighbours, nb, 3), local(counts, cnt, 4), local(colour, col, 5),
                local(pivot.at[0], mat_p0, 6), local(upper.at[0], mat_u, 7)]
        pl.semaphore_wait(barrier, jnp.where(s == last_line, 2, 3))

        @pl.when(s == 0)
        def _():
            start[0].start()
            start[2].start()

        first = [first_copies(side, (0, 2)) for side in (0, 1)]
        send_prev(first)
        for c in down:
            c.start()
        for c in mine:
            c.start()

        @pl.when(s == last_line)
        def _():
            send_prev_late(first)

        for c in mine:
            c.wait()
        own_part, far_first, solve_first, solve_second, alive, colours = make_solver()

        def term(j, t):
            part_t[tile(j), :] = jnp.where(colours == 0, alive[0] * t, v0[tile(j), :])

        def first0(j, t):
            cur0[tile(j), :] = part_t[tile(j), :] - jnp.where(colours == 0, alive[0] * t, 0.0)

        def keep(j, t):
            part_u[tile(j), :] = t

        def result(j, t):
            out[0, tile(j), :] = jnp.where(colours == 1, alive[0] * t, cur0[tile(j), :])

        up_early.wait_recv()
        for part in PARTS:
            landed(slow, part)
            far_first(got_y.at[0], part)
        again = []
        for kind, half in HALVES.items():
            begin = half.start // SUB
            products([(mat_p0, got_y.at[0])], term, masks, begin, begin + half.size // SUB)
            copies = again_copies(part_t, kind)
            start_slow_first(copies)
            again += copies
        down_t.start()
        for kind in HALVES:
            twin(part_t, kind, lambda c: c.start())
        up_x[0].wait_recv()
        products([(mat_u, got_x.at[0])], first0, masks)

        for kind in HALVES:
            twin(part_t, kind, lambda c: c.wait_send())
        finish_sends(first, again + down + [down_t])

        @pl.when(s == 0)
        def _():
            def second1(j, t):
                x1[1, tile(j), :] = alive[1] * t

            up[0].wait_recv()
            up[1].wait_recv()
            own_part(f0.at[1], r0, 0, cur0)
            up_cur.wait_recv()
            own_part(f1, r1, 1, cur1)
            up[2].wait_recv()
            up[3].wait_recv()
            solve_second(lambda: None, second1)
            products([(mat_p0, f0.at[1]), (mat_u, x1.at[1])], result, masks)
            start[0].wait_send()
            start[2].wait_send()

        @pl.when(s != 0)
        def _():
            up_y.wait_recv()
            products([(mat_p0, got_y.at[1])], keep, masks)
            up_x[1].wait_recv()
            products([(mat_u, got_x.at[1])], lambda j, t: result(j, part_u[tile(j), :] - t), masks)

    @pl.when(w == 1)
    def _():
        def greet(to, core):
            signal(barrier, to, core)

        @pl.when(s == last_line)
        def _():
            pl.semaphore_wait(barrier, 2)
            signal(ready.at[0], step2, 1)

        @pl.when(s == step1)
        def _():
            greet(0, 0)
            greet(0, 1)
            greet(step2, 1)

        @pl.when(s == step2)
        def _():
            greet(last_line, 1)

        greet(left, 0)
        greet(left, 1)
        greet(s, 0)

        @pl.when(s < last_line - 1)
        def _():
            greet(right, 0)
            greet(right, 1)

        mine = [local(prev.at[0], v1, 0), local(rhs.at[0], r1, 1), local(coupling.at[:, 0], c1, 2),
                local(neighbours, nb, 3), local(counts, cnt, 4), local(colour, col, 5),
                local(lower.at[0], mat_l, 6), local(pivot.at[0], mat_p1, 7)]

        @pl.when(s != last_line)
        def _():
            pl.semaphore_wait(barrier, jnp.where(s == step2, 3, 2))

        @pl.when(s == step2)
        def _():
            signal(ready.at[0], step1, 1)

        @pl.when(s == last_line - 1)
        def _():
            signal(ready.at[1], last_line, 1)

        @pl.when(s == 0)
        def _():
            start[1].start()

        first = [first_copies(side, (1,)) for side in (0, 1)]
        send_prev(first)
        for c in mine:
            c.start()

        @pl.when(s == last_line)
        def _():
            send_prev_late(first)

        def pass_on(arriving, leaving):
            pl.semaphore_wait(ready.at[0], 1)
            for part in order:
                arriving[part].wait_recv()
                leaving[part].start()

        @pl.when(s == step1)
        def _():
            pass_on(start, middle)

        @pl.when(s == step2)
        def _():
            pass_on(middle, end)

        for c in mine[:6]:
            c.wait()
        own_part, far_first, solve_first, solve_second, alive, colours = make_solver()
        own_part(f1, r1, 1, v1)
        for c in down[:3]:
            c.wait_recv()

        @pl.when(s == last_line)
        def _():
            signal(ready.at[1], last_line, 0)

        @pl.when(s == 0)
        def _():
            for c in up:
                c.start()

        own_part(f0.at[0], r0, 0, v0)
        mine[6].wait()
        mine[7].wait()

        def first1(j, t):
            x1[0, tile(j), :] = alive[1] * t
            cur1[tile(j), :] = jnp.where(colours == 0, alive[1] * t, v1[tile(j), :])

        def term(j, t):
            part_u[tile(j), :] = jnp.where(colours == 0, alive[0] * t, 0.0)

        def second1(j, t):
            x1[1, tile(j), :] = alive[1] * t
            out[0, tile(j), :] = jnp.where(colours == 1, alive[1] * t, cur1[tile(j), :])

        solve_first(first1)
        again1 = again_copies(cur1, 2)
        start_slow_first(again1)
        down[3].wait_recv()
        products([(mat_u, x1.at[0])], term, masks)
        again0 = again_copies(part_u, 1)
        start_slow_first(again0)
        up_x[0].start()
        own_part(f1, r1, 1, cur1)
        down_t.wait_recv()
        twin(cur1, 2, lambda c: c.start())
        twin(part_u, 1, lambda c: c.start())

        @pl.when(s == 0)
        def _():
            up_cur.start()

        def join(j, _):
            cur0[tile(j), :] = part_t[tile(j), :] - part_u[tile(j), :]
            return 0

        lax.fori_loop(0, TILES, join, 0, unroll=TILES)
        own_part(f0.at[1], r0, 0, cur0)

        twin(cur1, 2, lambda c: c.wait_send())
        twin(part_u, 1, lambda c: c.wait_send())
        finish_sends(first, [up_early, up_far[0], up_far[2], up_x[0]] + again0 + again1)

        @pl.when(s == 0)
        def _():
            for c in up + [up_cur]:
                c.wait_send()

        @pl.when(s == 0)
        def _():
            start[1].wait_send()

        @pl.when(s == step1)
        def _():
            for c in middle.values():
                c.wait_send()

        @pl.when(s == step2)
        def _():
            for c in end.values():
                c.wait_send()

        def after_y():
            @pl.when(s != 0)
            def _():
                up_y.start()

        solve_second(after_y, second1)

        @pl.when(s != 0)
        def _():
            up_x[1].start()

        @pl.when(s != 0)
        def _():
            up_y.wait_send()
            up_x[1].wait_send()


def shards(groups, rhs, prev_solution, lower, pivot_inv, upper_back, coupling, neighbours, counts, colour):
    plane = pltpu.VMEM((BLOCK, LANES), jnp.float32)
    matrix = pltpu.VMEM((BLOCK, BLOCK, LANES), jnp.float32)
    faces = pltpu.VMEM((FACES, BLOCK, LANES), jnp.float32)
    pair = pltpu.VMEM((2, BLOCK, LANES), jnp.float32)
    line = pltpu.VMEM((1, LANES), jnp.int32)
    dma = pltpu.SemaphoreType.DMA
    here = (rhs, prev_solution, lower, pivot_inv, upper_back, coupling, neighbours,
            counts.reshape(1, LANES), colour.reshape(1, LANES))
    return pl.pallas_call(
        functools.partial(kernel, groups),
        out_shape=pltpu.VMEM((1, BLOCK, LANES), jnp.float32),
        in_specs=[pl.BlockSpec(memory_space=pltpu.HBM)] * 9,
        out_specs=pl.BlockSpec(memory_space=pltpu.VMEM),
        scratch_shapes=[matrix] * 4 + [plane] * 4 + [faces] * 2
        + [pltpu.VMEM((FACES, LANES), jnp.int32), line, line]
        + [pltpu.VMEM((2, 2, BLOCK, LANES), jnp.float32), pltpu.VMEM((2, 3, BLOCK, LANES), jnp.float32), pair]
        + [plane, pair] + [plane] * 5 + [pair] * 3
        + [dma((8,)), dma((16,)), dma((14,)), dma((2, 3)), dma((2, 3)), dma((4, 2, 2)), dma((2, 4)), dma((3,)), dma((3,))]
        + [pltpu.SemaphoreType.REGULAR((2,))],
        compiler_params=pltpu.CompilerParams(collective_id=0, has_side_effects=True, vmem_limit_bytes=16 << 20),
    )(*[pltpu.with_memory_space_constraint(a, pltpu.HBM) for a in here])


def solution(mesh):
    placed = (
        P("wall", None, "surf"),
        P("wall", None, "surf"),
        P("wall", None, None, "surf"),
        P("wall", None, None, "surf"),
        P("wall", None, None, "surf"),
        P(None, "wall", None, "surf"),
        P(None, "surf"),
        P("surf"),
        P("surf"),
    )
    return jax.shard_map(
        functools.partial(shards, mesh.shape["surf"]), mesh=mesh, in_specs=placed, out_specs=P("wall", None, "surf"),
        check_vma=False,
    )
```

```python
import functools

import jax
import jax.numpy as jnp
from jax import lax
from jax.experimental import pallas as pl
from jax.experimental.pallas import tpu as pltpu
from jax.sharding import PartitionSpec as P

MESH = pl.DeviceIdType.MESH
BLOCK = 64
FACES = 4
LANES = 128
SUB = 8
TILES = BLOCK // SUB
HALVES = {0: pl.ds(0, BLOCK // 2), 3: pl.ds(BLOCK // 2, BLOCK // 2)}
PARTS = {0: HALVES[0], 2: HALVES[3]}
ROW = 4
PLANE = 16


def tile(j):
    return pl.ds(pl.multiple_of(j * SUB, SUB), SUB)


def fold(parts, masks):
    step = 1
    for mask in masks:
        merged = []
        for base in range(0, len(parts), 2):
            a, b = parts[base], parts[base + 1]
            merged.append(jnp.where(mask, a, b) + pltpu.roll(jnp.where(mask, b, a), step, 0))
        parts = merged
        step *= 2
    return parts[0]


def tree(terms):
    while len(terms) > 1:
        terms = [terms[i] + terms[i + 1] for i in range(0, len(terms) - 1, 2)] + terms[len(terms) & ~1:]
    return terms[0]


def products(pairs, finish, masks, first=0, last=TILES):
    vecs = [[vec[pl.ds(SUB * b, SUB), :] for b in range(TILES)] for _, vec in pairs]

    def body(j, _):
        parts = []
        for a in range(SUB):
            row = j * SUB + a
            terms = []
            for (mat, _), vec in zip(pairs, vecs):
                terms.append(tree([mat[row, pl.ds(SUB * b, SUB), :] * vec[b] for b in range(TILES)]))
            parts.append(terms[0] if len(terms) == 1 else terms[0] - terms[1])
        finish(j, fold(parts, masks))
        return 0

    lax.fori_loop(first, last, body, 0, unroll=last - first)


def kernel(groups, rhs, prev, lower, pivot, upper, coupling, neighbours, counts, colour, out,
           mat_l, mat_p1, mat_p0, mat_u, v0, v1, r0, r1, c0, c1, nb, cnt, col, h1, h2, f0, f1, x1, cur0, cur1, part_t, part_u, early,
           got_y, got_x, hop, loc, wsend, wrecv, s1, q1, s2, q2, rsend, rrecv, ready):
    s = lax.axis_index("surf")
    w = lax.axis_index("wall")
    right = lax.rem(s + 1, groups)
    left = lax.rem(s + groups - 1, groups)
    place = lax.rem(s, ROW)
    last_line = groups - 1
    sub = lax.broadcasted_iota(jnp.int32, (SUB, LANES), 0)
    masks = [(sub & 1) == 0, (sub & 2) == 0, (sub & 4) == 0]
    barrier = pltpu.get_barrier_semaphore()
    slow = jnp.where(place == ROW - 1, 1, 0)
    quick = 1 - slow
    slow_line = jnp.where(slow == 1, right, left)
    quick_line = jnp.where(slow == 1, left, right)

    def signal(sem, to, core):
        pl.semaphore_signal(sem, inc=1, device_id=(to, core), device_id_type=MESH)

    def local(src, dst, i):
        return pltpu.make_async_copy(src, dst, loc.at[i])

    def wall_copy(src, dst, i, to):
        return pltpu.make_async_remote_copy(src_ref=src, dst_ref=dst, send_sem=wsend.at[i], recv_sem=wrecv.at[i],
                                            device_id=(s, to), device_id_type=MESH)

    def piece(ref, part):
        return ref if part == 1 else ref.at[PARTS[part]]

    def first_copies(side, parts):
        return [pltpu.make_async_remote_copy(
            src_ref=piece(prev.at[0], part), dst_ref=piece(h1.at[side, part % 2], part), send_sem=s1.at[side, part],
            recv_sem=q1.at[side, part], device_id=(right if side == 0 else left, 1), device_id_type=MESH) for part in parts]

    def again_copy(src, kind, side, core):
        dst = h2.at[side, kind % 3]
        if kind in HALVES:
            src, dst = src.at[HALVES[kind]], dst.at[HALVES[kind]]
        return pltpu.make_async_remote_copy(
            src_ref=src, dst_ref=dst, send_sem=s2.at[kind, side, core], recv_sem=q2.at[side, kind],
            device_id=(right if side == 0 else left, core), device_id_type=MESH)

    def again_copies(src, kind):
        return [again_copy(src, kind, side, 1) for side in (0, 1)]

    def twin(src, kind, act):
        for source, side in ((last_line, 0), (1, 1)):
            @pl.when(s == source)
            def _():
                act(again_copy(src, kind, side, 0))

    down = [wall_copy(prev.at[0], v0, 0, 1), wall_copy(rhs.at[0], r0, 1, 1), wall_copy(coupling.at[:, 0], c0, 2, 1),
            wall_copy(upper.at[0], mat_u, 3, 1)]
    down_t = wall_copy(part_t, part_t, 4, 1)
    up = [wall_copy(rhs.at[0], r1, 5, 0), wall_copy(coupling.at[:, 0], c1, 6, 0), wall_copy(lower.at[0], mat_l, 7, 0),
          wall_copy(pivot.at[0], mat_p1, 8, 0)]
    up_cur = wall_copy(cur1, cur1, 9, 0)
    up_early = wall_copy(early, got_y.at[0], 10, 0)
    up_y = wall_copy(f0.at[1], got_y.at[1], 11, 0)
    up_far = {part: pltpu.make_async_remote_copy(
        src_ref=piece(h1.at[slow, 0], part), dst_ref=piece(h1.at[slow, 0], part), send_sem=wsend.at[14 + part // 2],
        recv_sem=q1.at[slow, part], device_id=(s, 0), device_id_type=MESH) for part in PARTS}
    up_x = [wall_copy(x1.at[i], got_x.at[i], 12 + i, 0) for i in (0, 1)]

    def start_slow_first(copies):
        @pl.when(place == 0)
        def _():
            copies[1].start()
            copies[0].start()

        @pl.when(place != 0)
        def _():
            copies[0].start()
            copies[1].start()

    def start_all(copies):
        for c in copies:
            c.start()

    def send_prev(copies):
        start_all(copies[0])

        @pl.when((s != 0) & (s != last_line))
        def _():
            start_all(copies[1])

    def send_prev_late(copies):
        pl.semaphore_wait(ready.at[1], 1)
        start_all(copies[1])

    step1, step2 = ROW - 1, PLANE - 1

    def relay(src, dst, part, to, recv):
        return pltpu.make_async_remote_copy(
            src_ref=piece(src, part), dst_ref=piece(dst, part), send_sem=rsend.at[part], recv_sem=recv, device_id=(to, 1),
            device_id_type=MESH)

    order = (0, 2, 1)
    start = {part: relay(prev.at[0], hop.at[part % 2], part, step1, rrecv.at[part]) for part in order}
    middle = {part: relay(hop.at[part % 2], hop.at[part % 2], part, step2, rrecv.at[part]) for part in order}
    end = {part: relay(hop.at[part % 2], h1.at[1, part % 2], part, last_line, q1.at[1, part]) for part in order}

    def finish_sends(first, others):
        for c in first[0] + others:
            c.wait_send()

        @pl.when(s != 0)
        def _():
            for c in first[1]:
                c.wait_send()

    def landed(side, part):
        ref = piece(h1.at[side, part % 2], part)
        pltpu.make_async_copy(ref, ref, q1.at[side, part]).wait()

    def arrived(buf, recv, side, kind, half=None):
        ref = buf.at[side, kind % 3]
        if half is not None:
            ref = ref.at[half]
        pltpu.make_async_copy(ref, ref, recv.at[side, kind]).wait()

    def make_solver():
        owners = ([], [], [])
        lanes = []
        for k in range(FACES):
            line = nb[pl.ds(k, 1), :]
            lanes.append(jnp.broadcast_to(line & (LANES - 1), (SUB, LANES)))
            owner = jnp.broadcast_to(line >> 7, (SUB, LANES))
            for masks_of, holder in zip(owners, (s, quick_line, slow_line)):
                masks_of.append(owner == holder)
        here, near, far = owners
        alive = [jnp.broadcast_to((cnt[...] > row).astype(jnp.float32), (SUB, LANES)) for row in (0, 1)]
        colours = jnp.broadcast_to(col[...], (SUB, LANES))
        coef = (c0, c1)

        def minus(begin, row, j, value, held_by, sign):
            for k in range(FACES):
                taken = jnp.take_along_axis(value, lanes[k], axis=1, mode="promise_in_bounds")
                term = coef[row][k, tile(j), :] * jnp.where(held_by[k], taken, 0.0)
                begin = begin + term if sign > 0 else begin - term
            return begin

        def own_part(total, given, row, field):
            def body(j, _):
                total[tile(j), :] = minus(given[tile(j), :], row, j, field[tile(j), :], here, -1)
                return 0

            lax.fori_loop(0, TILES, body, 0, unroll=TILES)

        def take(total, buf, recv, side, kind, held_by, row, sign, scale=None, half=None):
            arrived(buf, recv, side, kind, half)

            def body(j, _):
                value = minus(total[tile(j), :], row, j, buf[side, kind % 3, tile(j), :], held_by, sign)
                total[tile(j), :] = value if scale is None else scale * value
                return 0

            begin = 0 if half is None else half.start // SUB
            count = TILES if half is None else half.size // SUB
            lax.fori_loop(begin, begin + count, body, 0, unroll=count)

        def take_first(total, side, held_by, part, scale=None):
            row = part % 2

            def body(j, _):
                value = minus(total[tile(j), :], row, j, h1[side, row, tile(j), :], held_by, -1)
                total[tile(j), :] = value if scale is None else scale * value
                return 0

            begin = 0 if part == 1 else PARTS[part].start // SUB
            count = TILES if part == 1 else PARTS[part].size // SUB
            lax.fori_loop(begin, begin + count, body, 0, unroll=count)

        def far_first(total, part):
            take_first(total, slow, far, part, alive[0])

        def solve_first(finish):
            y0 = f0.at[0]
            for part in PARTS:
                landed(quick, part)
                take_first(y0, quick, near, part)
            early[...] = y0[...]
            up_early.start()
            landed(quick, 1)
            take_first(f1, quick, near, 1)
            for part in PARTS:
                landed(slow, part)
                up_far[part].start()
                far_first(y0, part)
            landed(slow, 1)

            def forward(j, t):
                source = minus(f1[tile(j), :], 1, j, h1[slow, 1, tile(j), :], far, -1)
                f1[tile(j), :] = alive[1] * (source - t)

            products([(mat_l, y0)], forward, masks)
            products([(mat_p1, f1)], finish, masks)

        def solve_second(after_y, finish):
            y0 = f0.at[1]

            def forward(j, t):
                early[tile(j), :] = alive[1] * (f1[tile(j), :] - t)

            def run(turn, _):
                @pl.when(turn == 1)
                def _():
                    for side, held_by in ((quick, near), (slow, far)):
                        take(f1, h2, q2, side, 2, held_by, 1, -1)
                        take(y0, h2, q2, side, 1, held_by, 0, 1)
                        for kind, half in HALVES.items():
                            take(y0, h2, q2, side, kind, held_by, 0, -1, alive[0] if held_by is far else None, half)
                    after_y()

                products([(mat_l, y0)], forward, masks)
                products([(mat_p1, early)], finish, masks)
                return 0

            lax.fori_loop(0, 2, run, 0)

        return own_part, far_first, solve_first, solve_second, alive, colours

    @pl.when(w == 0)
    def _():
        mine = [local(prev.at[0], v0, 0), local(rhs.at[0], r0, 1), local(coupling.at[:, 0], c0, 2),
                local(neighbours, nb, 3), local(counts, cnt, 4), local(colour, col, 5),
                local(pivot.at[0], mat_p0, 6), local(upper.at[0], mat_u, 7)]
        pl.semaphore_wait(barrier, jnp.where(s == last_line, 2, 3))

        @pl.when(s == 0)
        def _():
            start[0].start()
            start[2].start()

        first = [first_copies(side, (0, 2)) for side in (0, 1)]
        send_prev(first)
        for c in down:
            c.start()
        for c in mine:
            c.start()

        @pl.when(s == last_line)
        def _():
            send_prev_late(first)

        for c in mine:
            c.wait()
        own_part, far_first, solve_first, solve_second, alive, colours = make_solver()

        def term(j, t):
            part_t[tile(j), :] = jnp.where(colours == 0, alive[0] * t, v0[tile(j), :])

        def first0(j, t):
            cur0[tile(j), :] = part_t[tile(j), :] - jnp.where(colours == 0, alive[0] * t, 0.0)

        def keep(j, t):
            part_u[tile(j), :] = t

        def result(j, t):
            out[0, tile(j), :] = jnp.where(colours == 1, alive[0] * t, cur0[tile(j), :])

        def run(turn, _):
            @pl.when(turn == 1)
            def _():
                up_early.wait_recv()
                f0[0] = got_y[0]
                for part in PARTS:
                    landed(slow, part)
                    far_first(f0.at[0], part)

            for kind, half in HALVES.items():
                begin = half.start // SUB
                products([(mat_p0, f0.at[0])], term, masks, begin, begin + half.size // SUB)

                @pl.when(turn == 1)
                def _():
                    start_slow_first(again_copies(part_t, kind))

            return 0

        f0[0] = v0[...]
        lax.fori_loop(0, 2, run, 0)
        again = again_copies(part_t, 0) + again_copies(part_t, 3)
        down_t.start()
        for kind in HALVES:
            twin(part_t, kind, lambda c: c.start())
        up_x[0].wait_recv()
        products([(mat_u, got_x.at[0])], first0, masks)

        for kind in HALVES:
            twin(part_t, kind, lambda c: c.wait_send())
        finish_sends(first, again + down + [down_t])

        @pl.when(s == 0)
        def _():
            def second1(j, t):
                x1[1, tile(j), :] = alive[1] * t

            up[0].wait_recv()
            up[1].wait_recv()
            own_part(f0.at[1], r0, 0, cur0)
            up_cur.wait_recv()
            own_part(f1, r1, 1, cur1)
            up[2].wait_recv()
            up[3].wait_recv()
            solve_second(lambda: None, second1)
            products([(mat_p0, f0.at[1]), (mat_u, x1.at[1])], result, masks)
            start[0].wait_send()
            start[2].wait_send()

        @pl.when(s != 0)
        def _():
            up_y.wait_recv()
            products([(mat_p0, got_y.at[1])], keep, masks)
            up_x[1].wait_recv()
            products([(mat_u, got_x.at[1])], lambda j, t: result(j, part_u[tile(j), :] - t), masks)

    @pl.when(w == 1)
    def _():
        def greet(to, core):
            signal(barrier, to, core)

        @pl.when(s == last_line)
        def _():
            pl.semaphore_wait(barrier, 2)
            signal(ready.at[0], step2, 1)

        @pl.when(s == step1)
        def _():
            greet(0, 0)
            greet(0, 1)
            greet(step2, 1)

        @pl.when(s == step2)
        def _():
            greet(last_line, 1)

        greet(left, 0)
        greet(left, 1)
        greet(s, 0)

        @pl.when(s < last_line - 1)
        def _():
            greet(right, 0)
            greet(right, 1)

        mine = [local(prev.at[0], v1, 0), local(rhs.at[0], r1, 1), local(coupling.at[:, 0], c1, 2),
                local(neighbours, nb, 3), local(counts, cnt, 4), local(colour, col, 5),
                local(lower.at[0], mat_l, 6), local(pivot.at[0], mat_p1, 7)]

        @pl.when(s != last_line)
        def _():
            pl.semaphore_wait(barrier, jnp.where(s == step2, 3, 2))

        @pl.when(s == step2)
        def _():
            signal(ready.at[0], step1, 1)

        @pl.when(s == last_line - 1)
        def _():
            signal(ready.at[1], last_line, 1)

        @pl.when(s == 0)
        def _():
            start[1].start()

        first = [first_copies(side, (1,)) for side in (0, 1)]
        send_prev(first)
        for c in mine:
            c.start()

        @pl.when(s == last_line)
        def _():
            send_prev_late(first)

        def pass_on(arriving, leaving):
            pl.semaphore_wait(ready.at[0], 1)
            for part in order:
                arriving[part].wait_recv()
                leaving[part].start()

        @pl.when(s == step1)
        def _():
            pass_on(start, middle)

        @pl.when(s == step2)
        def _():
            pass_on(middle, end)

        for c in mine[:6]:
            c.wait()
        own_part, far_first, solve_first, solve_second, alive, colours = make_solver()
        own_part(f1, r1, 1, v1)
        for c in down[:3]:
            c.wait_recv()

        @pl.when(s == last_line)
        def _():
            signal(ready.at[1], last_line, 0)

        @pl.when(s == 0)
        def _():
            for c in up:
                c.start()

        own_part(f0.at[0], r0, 0, v0)
        mine[6].wait()
        mine[7].wait()

        def first1(j, t):
            x1[0, tile(j), :] = alive[1] * t
            cur1[tile(j), :] = jnp.where(colours == 0, alive[1] * t, v1[tile(j), :])

        def term(j, t):
            part_u[tile(j), :] = jnp.where(colours == 0, alive[0] * t, 0.0)

        def second1(j, t):
            x1[1, tile(j), :] = alive[1] * t
            out[0, tile(j), :] = jnp.where(colours == 1, alive[1] * t, cur1[tile(j), :])

        solve_first(first1)
        again1 = again_copies(cur1, 2)
        start_slow_first(again1)
        down[3].wait_recv()
        products([(mat_u, x1.at[0])], term, masks)
        again0 = again_copies(part_u, 1)
        start_slow_first(again0)
        up_x[0].start()
        own_part(f1, r1, 1, cur1)
        down_t.wait_recv()
        twin(cur1, 2, lambda c: c.start())
        twin(part_u, 1, lambda c: c.start())

        @pl.when(s == 0)
        def _():
            up_cur.start()

        def join(j, _):
            cur0[tile(j), :] = part_t[tile(j), :] - part_u[tile(j), :]
            return 0

        lax.fori_loop(0, TILES, join, 0, unroll=TILES)
        own_part(f0.at[1], r0, 0, cur0)

        twin(cur1, 2, lambda c: c.wait_send())
        twin(part_u, 1, lambda c: c.wait_send())
        finish_sends(first, [up_early, up_far[0], up_far[2], up_x[0]] + again0 + again1)

        @pl.when(s == 0)
        def _():
            for c in up + [up_cur]:
                c.wait_send()

        @pl.when(s == 0)
        def _():
            start[1].wait_send()

        @pl.when(s == step1)
        def _():
            for c in middle.values():
                c.wait_send()

        @pl.when(s == step2)
        def _():
            for c in end.values():
                c.wait_send()

        def after_y():
            @pl.when(s != 0)
            def _():
                up_y.start()

        solve_second(after_y, second1)

        @pl.when(s != 0)
        def _():
            up_x[1].start()

        @pl.when(s != 0)
        def _():
            up_y.wait_send()
            up_x[1].wait_send()


def shards(groups, rhs, prev_solution, lower, pivot_inv, upper_back, coupling, neighbours, counts, colour):
    plane = pltpu.VMEM((BLOCK, LANES), jnp.float32)
    matrix = pltpu.VMEM((BLOCK, BLOCK, LANES), jnp.float32)
    faces = pltpu.VMEM((FACES, BLOCK, LANES), jnp.float32)
    pair = pltpu.VMEM((2, BLOCK, LANES), jnp.float32)
    line = pltpu.VMEM((1, LANES), jnp.int32)
    dma = pltpu.SemaphoreType.DMA
    here = (rhs, prev_solution, lower, pivot_inv, upper_back, coupling, neighbours,
            counts.reshape(1, LANES), colour.reshape(1, LANES))
    return pl.pallas_call(
        functools.partial(kernel, groups),
        out_shape=pltpu.VMEM((1, BLOCK, LANES), jnp.float32),
        in_specs=[pl.BlockSpec(memory_space=pltpu.HBM)] * 9,
        out_specs=pl.BlockSpec(memory_space=pltpu.VMEM),
        scratch_shapes=[matrix] * 4 + [plane] * 4 + [faces] * 2
        + [pltpu.VMEM((FACES, LANES), jnp.int32), line, line]
        + [pltpu.VMEM((2, 2, BLOCK, LANES), jnp.float32), pltpu.VMEM((2, 3, BLOCK, LANES), jnp.float32), pair]
        + [plane, pair] + [plane] * 5 + [pair] * 3
        + [dma((8,)), dma((16,)), dma((14,)), dma((2, 3)), dma((2, 3)), dma((4, 2, 2)), dma((2, 4)), dma((3,)), dma((3,))]
        + [pltpu.SemaphoreType.REGULAR((2,))],
        compiler_params=pltpu.CompilerParams(collective_id=0, has_side_effects=True, vmem_limit_bytes=16 << 20),
    )(*[pltpu.with_memory_space_constraint(a, pltpu.HBM) for a in here])


def solution(mesh):
    placed = (
        P("wall", None, "surf"),
        P("wall", None, "surf"),
        P("wall", None, None, "surf"),
        P("wall", None, None, "surf"),
        P("wall", None, None, "surf"),
        P(None, "wall", None, "surf"),
        P(None, "surf"),
        P("surf"),
        P("surf"),
    )
    return jax.shard_map(
        functools.partial(shards, mesh.shape["surf"]), mesh=mesh, in_specs=placed, out_specs=P("wall", None, "surf"),
        check_vma=False,
    )
```

```python
import functools

import jax
import jax.numpy as jnp
from jax import lax
from jax.experimental import pallas as pl
from jax.experimental.pallas import tpu as pltpu
from jax.sharding import PartitionSpec as P

MESH = pl.DeviceIdType.MESH
BLOCK = 64
FACES = 4
LANES = 128
SUB = 8
TILES = BLOCK // SUB
HALVES = {0: pl.ds(0, BLOCK // 2), 3: pl.ds(BLOCK // 2, BLOCK // 2)}
PARTS = {0: HALVES[0], 2: HALVES[3]}
ROW = 4
PLANE = 16


def tile(j):
    return pl.ds(pl.multiple_of(j * SUB, SUB), SUB)


def fold(parts, masks):
    step = 1
    for mask in masks:
        merged = []
        for base in range(0, len(parts), 2):
            a, b = parts[base], parts[base + 1]
            merged.append(jnp.where(mask, a, b) + pltpu.roll(jnp.where(mask, b, a), step, 0))
        parts = merged
        step *= 2
    return parts[0]


def tree(terms):
    while len(terms) > 1:
        terms = [terms[i] + terms[i + 1] for i in range(0, len(terms) - 1, 2)] + terms[len(terms) & ~1:]
    return terms[0]


def products(pairs, finish, masks, first=0, last=TILES):
    vecs = [[vec[pl.ds(SUB * b, SUB), :] for b in range(TILES)] for _, vec in pairs]

    def body(j, _):
        parts = []
        for a in range(SUB):
            row = j * SUB + a
            terms = []
            for (mat, _), vec in zip(pairs, vecs):
                terms.append(tree([mat[row, pl.ds(SUB * b, SUB), :] * vec[b] for b in range(TILES)]))
            parts.append(terms[0] if len(terms) == 1 else terms[0] - terms[1])
        finish(j, fold(parts, masks))
        return 0

    lax.fori_loop(first, last, body, 0, unroll=last - first)


def kernel(groups, rhs, prev, lower, pivot, upper, coupling, neighbours, counts, colour, out,
           mat_l, mat_p1, mat_p0, mat_u, v0, v1, r0, r1, c0, c1, nb, cnt, col, h1, h2, f0, f1, x1, cur0, cur1, part_t, part_u, early,
           got_y, got_x, hop, loc, wsend, wrecv, s1, q1, s2, q2, rsend, rrecv, ready):
    s = lax.axis_index("surf")
    w = lax.axis_index("wall")
    right = lax.rem(s + 1, groups)
    left = lax.rem(s + groups - 1, groups)
    place = lax.rem(s, ROW)
    last_line = groups - 1
    sub = lax.broadcasted_iota(jnp.int32, (SUB, LANES), 0)
    masks = [(sub & 1) == 0, (sub & 2) == 0, (sub & 4) == 0]
    barrier = pltpu.get_barrier_semaphore()
    slow = jnp.where(place == ROW - 1, 1, 0)
    quick = 1 - slow
    slow_line = jnp.where(slow == 1, right, left)
    quick_line = jnp.where(slow == 1, left, right)

    def signal(sem, to, core):
        pl.semaphore_signal(sem, inc=1, device_id=(to, core), device_id_type=MESH)

    def local(src, dst, i):
        return pltpu.make_async_copy(src, dst, loc.at[i])

    def wall_copy(src, dst, i, to):
        return pltpu.make_async_remote_copy(src_ref=src, dst_ref=dst, send_sem=wsend.at[i], recv_sem=wrecv.at[i],
                                            device_id=(s, to), device_id_type=MESH)

    def piece(ref, part):
        return ref if part == 1 else ref.at[PARTS[part]]

    def first_copies(side, parts):
        return [pltpu.make_async_remote_copy(
            src_ref=piece(prev.at[0], part), dst_ref=piece(h1.at[side, part % 2], part), send_sem=s1.at[side, part],
            recv_sem=q1.at[side, part], device_id=(right if side == 0 else left, 1), device_id_type=MESH) for part in parts]

    def again_copy(src, kind, side, core):
        dst = h2.at[side, kind % 3]
        if kind in HALVES:
            src, dst = src.at[HALVES[kind]], dst.at[HALVES[kind]]
        return pltpu.make_async_remote_copy(
            src_ref=src, dst_ref=dst, send_sem=s2.at[kind, side, core], recv_sem=q2.at[side, kind],
            device_id=(right if side == 0 else left, core), device_id_type=MESH)

    def again_copies(src, kind):
        return [again_copy(src, kind, side, 1) for side in (0, 1)]

    def twin(src, kind, act):
        for source, side in ((last_line, 0), (1, 1)):
            @pl.when(s == source)
            def _():
                act(again_copy(src, kind, side, 0))

    down = [wall_copy(prev.at[0], v0, 0, 1), wall_copy(rhs.at[0], r0, 1, 1), wall_copy(coupling.at[:, 0], c0, 2, 1),
            wall_copy(upper.at[0], mat_u, 3, 1)]
    down_t = wall_copy(part_t, part_t, 4, 1)
    up = [wall_copy(rhs.at[0], r1, 5, 0), wall_copy(coupling.at[:, 0], c1, 6, 0), wall_copy(lower.at[0], mat_l, 7, 0),
          wall_copy(pivot.at[0], mat_p1, 8, 0)]
    up_cur = wall_copy(cur1, cur1, 9, 0)
    up_early = wall_copy(early, got_y.at[0], 10, 0)
    up_y = wall_copy(f0.at[1], got_y.at[1], 11, 0)
    def up_raw(side, first_sem):
        return {part: pltpu.make_async_remote_copy(
            src_ref=piece(h1.at[side, 0], part), dst_ref=piece(h1.at[side, 0], part), send_sem=wsend.at[first_sem + part // 2],
            recv_sem=q1.at[side, part], device_id=(s, 0), device_id_type=MESH) for part in PARTS}

    up_far = up_raw(slow, 14)
    up_near = up_raw(quick, 16)
    up_x = [wall_copy(x1.at[i], got_x.at[i], 12 + i, 0) for i in (0, 1)]

    def start_slow_first(copies):
        @pl.when(place == 0)
        def _():
            copies[1].start()
            copies[0].start()

        @pl.when(place != 0)
        def _():
            copies[0].start()
            copies[1].start()

    def start_all(copies):
        for c in copies:
            c.start()

    def send_prev(copies):
        start_all(copies[0])

        @pl.when((s != 0) & (s != last_line))
        def _():
            start_all(copies[1])

    def send_prev_late(copies):
        pl.semaphore_wait(ready.at[1], 1)
        start_all(copies[1])

    step1, step2 = ROW - 1, PLANE - 1

    def relay(src, dst, part, to, recv):
        return pltpu.make_async_remote_copy(
            src_ref=piece(src, part), dst_ref=piece(dst, part), send_sem=rsend.at[part], recv_sem=recv, device_id=(to, 1),
            device_id_type=MESH)

    order = (0, 2, 1)
    start = {part: relay(prev.at[0], hop.at[part % 2], part, step1, rrecv.at[part]) for part in order}
    middle = {part: relay(hop.at[part % 2], hop.at[part % 2], part, step2, rrecv.at[part]) for part in order}
    end = {part: relay(hop.at[part % 2], h1.at[1, part % 2], part, last_line, q1.at[1, part]) for part in order}

    def finish_sends(first, others):
        for c in first[0] + others:
            c.wait_send()

        @pl.when(s != 0)
        def _():
            for c in first[1]:
                c.wait_send()

    def landed(side, part):
        ref = piece(h1.at[side, part % 2], part)
        pltpu.make_async_copy(ref, ref, q1.at[side, part]).wait()

    def arrived(buf, recv, side, kind, half=None):
        ref = buf.at[side, kind % 3]
        if half is not None:
            ref = ref.at[half]
        pltpu.make_async_copy(ref, ref, recv.at[side, kind]).wait()

    def make_solver():
        owners = ([], [], [])
        lanes = []
        for k in range(FACES):
            line = nb[pl.ds(k, 1), :]
            lanes.append(jnp.broadcast_to(line & (LANES - 1), (SUB, LANES)))
            owner = jnp.broadcast_to(line >> 7, (SUB, LANES))
            for masks_of, holder in zip(owners, (s, quick_line, slow_line)):
                masks_of.append(owner == holder)
        here, near, far = owners
        alive = [jnp.broadcast_to((cnt[...] > row).astype(jnp.float32), (SUB, LANES)) for row in (0, 1)]
        colours = jnp.broadcast_to(col[...], (SUB, LANES))
        coef = (c0, c1)

        def minus(begin, row, j, value, held_by, sign):
            for k in range(FACES):
                taken = jnp.take_along_axis(value, lanes[k], axis=1, mode="promise_in_bounds")
                term = coef[row][k, tile(j), :] * jnp.where(held_by[k], taken, 0.0)
                begin = begin + term if sign > 0 else begin - term
            return begin

        def own_part(total, given, row, field):
            def body(j, _):
                total[tile(j), :] = minus(given[tile(j), :], row, j, field[tile(j), :], here, -1)
                return 0

            lax.fori_loop(0, TILES, body, 0, unroll=TILES)

        def take(total, buf, recv, side, kind, held_by, row, sign, scale=None, half=None):
            arrived(buf, recv, side, kind, half)

            def body(j, _):
                value = minus(total[tile(j), :], row, j, buf[side, kind % 3, tile(j), :], held_by, sign)
                total[tile(j), :] = value if scale is None else scale * value
                return 0

            begin = 0 if half is None else half.start // SUB
            count = TILES if half is None else half.size // SUB
            lax.fori_loop(begin, begin + count, body, 0, unroll=count)

        def take_first(total, side, held_by, part, scale=None):
            row = part % 2

            def body(j, _):
                value = minus(total[tile(j), :], row, j, h1[side, row, tile(j), :], held_by, -1)
                total[tile(j), :] = value if scale is None else scale * value
                return 0

            begin = 0 if part == 1 else PARTS[part].start // SUB
            count = TILES if part == 1 else PARTS[part].size // SUB
            lax.fori_loop(begin, begin + count, body, 0, unroll=count)

        def near_first(total, part):
            take_first(total, quick, near, part)

        def far_first(total, part):
            take_first(total, slow, far, part, alive[0])

        def solve_first(finish):
            y0 = f0.at[0]
            early[...] = y0[...]
            up_early.start()
            for part in PARTS:
                landed(quick, part)
                up_near[part].start()
                take_first(y0, quick, near, part)
            landed(quick, 1)
            take_first(f1, quick, near, 1)
            for part in PARTS:
                landed(slow, part)
                up_far[part].start()
                far_first(y0, part)
            landed(slow, 1)

            def forward(j, t):
                source = minus(f1[tile(j), :], 1, j, h1[slow, 1, tile(j), :], far, -1)
                f1[tile(j), :] = alive[1] * (source - t)

            products([(mat_l, y0)], forward, masks)
            products([(mat_p1, f1)], finish, masks)

        def solve_second(after_y, finish):
            y0 = f0.at[1]

            def forward(j, t):
                early[tile(j), :] = alive[1] * (f1[tile(j), :] - t)

            def run(turn, _):
                @pl.when(turn == 1)
                def _():
                    for side, held_by in ((quick, near), (slow, far)):
                        take(f1, h2, q2, side, 2, held_by, 1, -1)
                        take(y0, h2, q2, side, 1, held_by, 0, 1)
                        for kind, half in HALVES.items():
                            take(y0, h2, q2, side, kind, held_by, 0, -1, alive[0] if held_by is far else None, half)
                    after_y()

                products([(mat_l, y0)], forward, masks)
                products([(mat_p1, early)], finish, masks)
                return 0

            lax.fori_loop(0, 2, run, 0)

        return own_part, near_first, far_first, solve_first, solve_second, alive, colours

    @pl.when(w == 0)
    def _():
        mine = [local(prev.at[0], v0, 0), local(rhs.at[0], r0, 1), local(coupling.at[:, 0], c0, 2),
                local(neighbours, nb, 3), local(counts, cnt, 4), local(colour, col, 5),
                local(pivot.at[0], mat_p0, 6), local(upper.at[0], mat_u, 7)]
        pl.semaphore_wait(barrier, jnp.where(s == last_line, 2, 3))

        @pl.when(s == 0)
        def _():
            start[0].start()
            start[2].start()

        first = [first_copies(side, (0, 2)) for side in (0, 1)]
        send_prev(first)
        for c in down:
            c.start()
        for c in mine:
            c.start()

        @pl.when(s == last_line)
        def _():
            send_prev_late(first)

        for c in mine:
            c.wait()
        own_part, near_first, far_first, solve_first, solve_second, alive, colours = make_solver()

        def term(j, t):
            part_t[tile(j), :] = jnp.where(colours == 0, alive[0] * t, v0[tile(j), :])

        def first0(j, t):
            cur0[tile(j), :] = part_t[tile(j), :] - jnp.where(colours == 0, alive[0] * t, 0.0)

        def keep(j, t):
            part_u[tile(j), :] = t

        def result(j, t):
            out[0, tile(j), :] = jnp.where(colours == 1, alive[0] * t, cur0[tile(j), :])

        def run(turn, _):
            @pl.when(turn == 1)
            def _():
                up_early.wait_recv()
                f0[0] = got_y[0]
                for part in PARTS:
                    landed(quick, part)
                    near_first(f0.at[0], part)
                for part in PARTS:
                    landed(slow, part)
                    far_first(f0.at[0], part)

            for kind, half in HALVES.items():
                begin = half.start // SUB
                products([(mat_p0, f0.at[0])], term, masks, begin, begin + half.size // SUB)

                @pl.when(turn == 1)
                def _():
                    start_slow_first(again_copies(part_t, kind))

            return 0

        f0[0] = v0[...]
        lax.fori_loop(0, 2, run, 0)
        again = again_copies(part_t, 0) + again_copies(part_t, 3)
        down_t.start()
        for kind in HALVES:
            twin(part_t, kind, lambda c: c.start())
        up_x[0].wait_recv()
        products([(mat_u, got_x.at[0])], first0, masks)

        for kind in HALVES:
            twin(part_t, kind, lambda c: c.wait_send())
        finish_sends(first, again + down + [down_t])

        @pl.when(s == 0)
        def _():
            def second1(j, t):
                x1[1, tile(j), :] = alive[1] * t

            up[0].wait_recv()
            up[1].wait_recv()
            own_part(f0.at[1], r0, 0, cur0)
            up_cur.wait_recv()
            own_part(f1, r1, 1, cur1)
            up[2].wait_recv()
            up[3].wait_recv()
            solve_second(lambda: None, second1)
            products([(mat_p0, f0.at[1]), (mat_u, x1.at[1])], result, masks)
            start[0].wait_send()
            start[2].wait_send()

        @pl.when(s != 0)
        def _():
            up_y.wait_recv()
            products([(mat_p0, got_y.at[1])], keep, masks)
            up_x[1].wait_recv()
            products([(mat_u, got_x.at[1])], lambda j, t: result(j, part_u[tile(j), :] - t), masks)

    @pl.when(w == 1)
    def _():
        def greet(to, core):
            signal(barrier, to, core)

        @pl.when(s == last_line)
        def _():
            pl.semaphore_wait(barrier, 2)
            signal(ready.at[0], step2, 1)

        @pl.when(s == step1)
        def _():
            greet(0, 0)
            greet(0, 1)
            greet(step2, 1)

        @pl.when(s == step2)
        def _():
            greet(last_line, 1)

        greet(left, 0)
        greet(left, 1)
        greet(s, 0)

        @pl.when(s < last_line - 1)
        def _():
            greet(right, 0)
            greet(right, 1)

        mine = [local(prev.at[0], v1, 0), local(rhs.at[0], r1, 1), local(coupling.at[:, 0], c1, 2),
                local(neighbours, nb, 3), local(counts, cnt, 4), local(colour, col, 5),
                local(lower.at[0], mat_l, 6), local(pivot.at[0], mat_p1, 7)]

        @pl.when(s != last_line)
        def _():
            pl.semaphore_wait(barrier, jnp.where(s == step2, 3, 2))

        @pl.when(s == step2)
        def _():
            signal(ready.at[0], step1, 1)

        @pl.when(s == last_line - 1)
        def _():
            signal(ready.at[1], last_line, 1)

        @pl.when(s == 0)
        def _():
            start[1].start()

        first = [first_copies(side, (1,)) for side in (0, 1)]
        send_prev(first)
        for c in mine:
            c.start()

        @pl.when(s == last_line)
        def _():
            send_prev_late(first)

        def pass_on(arriving, leaving):
            pl.semaphore_wait(ready.at[0], 1)
            for part in order:
                arriving[part].wait_recv()
                leaving[part].start()

        @pl.when(s == step1)
        def _():
            pass_on(start, middle)

        @pl.when(s == step2)
        def _():
            pass_on(middle, end)

        for c in mine[:6]:
            c.wait()
        own_part, near_first, far_first, solve_first, solve_second, alive, colours = make_solver()
        own_part(f1, r1, 1, v1)
        for c in down[:3]:
            c.wait_recv()

        @pl.when(s == last_line)
        def _():
            signal(ready.at[1], last_line, 0)

        @pl.when(s == 0)
        def _():
            for c in up:
                c.start()

        own_part(f0.at[0], r0, 0, v0)
        mine[6].wait()
        mine[7].wait()

        def first1(j, t):
            x1[0, tile(j), :] = alive[1] * t
            cur1[tile(j), :] = jnp.where(colours == 0, alive[1] * t, v1[tile(j), :])

        def term(j, t):
            part_u[tile(j), :] = jnp.where(colours == 0, alive[0] * t, 0.0)

        def second1(j, t):
            x1[1, tile(j), :] = alive[1] * t
            out[0, tile(j), :] = jnp.where(colours == 1, alive[1] * t, cur1[tile(j), :])

        solve_first(first1)
        again1 = again_copies(cur1, 2)
        start_slow_first(again1)
        down[3].wait_recv()
        products([(mat_u, x1.at[0])], term, masks)
        again0 = again_copies(part_u, 1)
        start_slow_first(again0)
        up_x[0].start()
        own_part(f1, r1, 1, cur1)
        down_t.wait_recv()
        twin(cur1, 2, lambda c: c.start())
        twin(part_u, 1, lambda c: c.start())

        @pl.when(s == 0)
        def _():
            up_cur.start()

        def join(j, _):
            cur0[tile(j), :] = part_t[tile(j), :] - part_u[tile(j), :]
            return 0

        lax.fori_loop(0, TILES, join, 0, unroll=TILES)
        own_part(f0.at[1], r0, 0, cur0)

        twin(cur1, 2, lambda c: c.wait_send())
        twin(part_u, 1, lambda c: c.wait_send())
        finish_sends(first, [up_early, up_near[0], up_near[2], up_far[0], up_far[2], up_x[0]] + again0 + again1)

        @pl.when(s == 0)
        def _():
            for c in up + [up_cur]:
                c.wait_send()

        @pl.when(s == 0)
        def _():
            start[1].wait_send()

        @pl.when(s == step1)
        def _():
            for c in middle.values():
                c.wait_send()

        @pl.when(s == step2)
        def _():
            for c in end.values():
                c.wait_send()

        def after_y():
            @pl.when(s != 0)
            def _():
                up_y.start()

        solve_second(after_y, second1)

        @pl.when(s != 0)
        def _():
            up_x[1].start()

        @pl.when(s != 0)
        def _():
            up_y.wait_send()
            up_x[1].wait_send()


def shards(groups, rhs, prev_solution, lower, pivot_inv, upper_back, coupling, neighbours, counts, colour):
    plane = pltpu.VMEM((BLOCK, LANES), jnp.float32)
    matrix = pltpu.VMEM((BLOCK, BLOCK, LANES), jnp.float32)
    faces = pltpu.VMEM((FACES, BLOCK, LANES), jnp.float32)
    pair = pltpu.VMEM((2, BLOCK, LANES), jnp.float32)
    line = pltpu.VMEM((1, LANES), jnp.int32)
    dma = pltpu.SemaphoreType.DMA
    here = (rhs, prev_solution, lower, pivot_inv, upper_back, coupling, neighbours,
            counts.reshape(1, LANES), colour.reshape(1, LANES))
    return pl.pallas_call(
        functools.partial(kernel, groups),
        out_shape=pltpu.VMEM((1, BLOCK, LANES), jnp.float32),
        in_specs=[pl.BlockSpec(memory_space=pltpu.HBM)] * 9,
        out_specs=pl.BlockSpec(memory_space=pltpu.VMEM),
        scratch_shapes=[matrix] * 4 + [plane] * 4 + [faces] * 2
        + [pltpu.VMEM((FACES, LANES), jnp.int32), line, line]
        + [pltpu.VMEM((2, 2, BLOCK, LANES), jnp.float32), pltpu.VMEM((2, 3, BLOCK, LANES), jnp.float32), pair]
        + [plane, pair] + [plane] * 5 + [pair] * 3
        + [dma((8,)), dma((18,)), dma((14,)), dma((2, 3)), dma((2, 3)), dma((4, 2, 2)), dma((2, 4)), dma((3,)), dma((3,))]
        + [pltpu.SemaphoreType.REGULAR((2,))],
        compiler_params=pltpu.CompilerParams(collective_id=0, has_side_effects=True, vmem_limit_bytes=16 << 20),
    )(*[pltpu.with_memory_space_constraint(a, pltpu.HBM) for a in here])


def solution(mesh):
    placed = (
        P("wall", None, "surf"),
        P("wall", None, "surf"),
        P("wall", None, None, "surf"),
        P("wall", None, None, "surf"),
        P("wall", None, None, "surf"),
        P(None, "wall", None, "surf"),
        P(None, "surf"),
        P("surf"),
        P("surf"),
    )
    return jax.shard_map(
        functools.partial(shards, mesh.shape["surf"]), mesh=mesh, in_specs=placed, out_specs=P("wall", None, "surf"),
        check_vma=False,
    )
```
